32 devices in a mesh: grp: 4 (over z), dev: 8 (over y, x, core).
Axes of the slice: x: 2, y: 2, z: 4, core: 2. Of those that a mesh axis runs over, the one named last changes fastest.
Arguments:
- output_gradient: bfloat16 [4096, 2048], P(('grp', 'dev')), may hold values from -6 to 6
- expert_choice_index: int32 [4096, 8], P(('grp', 'dev')), may hold values from 0 to 31, all different within a row; in each aligned block of 128 rows (0 to 127, 128 to 255, ...) at most 40 rows name the same one
- routing_weight: float32 [4096, 8], P(('grp', 'dev')), may hold values from 0.05 to 0.3
- stored_gate_preact: bfloat16 [32, 1280, 1536], P(('grp', 'dev')), may hold values from -6 to 6
- gate_up_weight: bfloat16 [32, 2048, 1536], P(('grp', 'dev')), may hold values from -0.125 to 0.125
- down_weight: bfloat16 [32, 768, 2048], P(('grp', 'dev')), may hold values from -0.21875 to 0.21875
- down_first_factor: bfloat16 [32, 64, 768], P(('grp', 'dev')), may hold values from -0.21875 to 0.21875
- down_second_factor: bfloat16 [32, 64, 2048], P(('grp', 'dev')), may hold values from -0.75 to 0.75
- rotated_queries: bfloat16 [4096, 4096], P('grp', 'dev'), may hold values from -800 to 800
- rotated_keys: bfloat16 [4096, 512], P('grp'), may hold values from -4 to 4
- stored_values: bfloat16 [4096, 512], P('grp'), may hold values from -6 to 6
- output_weight: bfloat16 [4096, 2048], P('dev'), may hold values from -0.09375 to 0.09375
- output_first_factor: bfloat16 [64, 4096], P(None, 'dev'), may hold values from -0.09375 to 0.09375
- output_second_factor: bfloat16 [64, 2048], replicated, may hold values from -0.75 to 0.75
Outputs:
- first_factor_gradient: float32 [32, 64, 768], P(('grp', 'dev'))
- second_factor_gradient: float32 [32, 64, 2048], P(('grp', 'dev'))
- residual_gradient: bfloat16 [4096, 2048], P(('grp', 'dev'))
- output_first_gradient: float32 [64, 4096], P(None, 'dev')
- output_second_gradient: float32 [64, 2048], replicated
- query_gradient: float32 [4096, 4096], P('grp', 'dev')
- key_gradient: float32 [4096, 512], P(('grp', 'dev'))
- value_gradient: float32 [4096, 512], P(('grp', 'dev'))
The draws below stay inside these ranges and needn't reach their ends.
Inputs may be any that keep to these rules, and one draw needn't show every extreme that they name: `expert_choice_index`: each row names 8 different experts; within the rows of one device no expert is named more than 40 times, a bound that some block reaches.
All inputs are finite; a program needn't handle non-finite values.
Results may differ from the reference program's by a relative error of at most 0.024.
Values may be sent and summed in bfloat16 or wider, within the bound.
No kernel may reach another device: no remote copies, remote signals or barrier semaphores. Data moves between devices by JAX's collectives and lax.ppermute only.
A program may use at most 192 MiB of HBM per device.

```python
import math
import jax
import jax.numpy as jnp
import numpy as np
from jax import lax

MODEL_DIM = 2048
FFN_HIDDEN = 768
QUERY_HEADS = 32
KVH = 4
HEAD_SIZE = 128
TOP = 8
ADAPTER_RANK = 64
TOK_DEV = 128
PIECE = 1024
TOKEN_TOTAL = 4096
EXPERT_COUNT = 32
CAP = 40
SLOTS = 1280
N_GRP = 4


def paired_states(key):
    shape_k = (TOKEN_TOTAL, KVH, HEAD_SIZE)
    shape_q = (TOKEN_TOTAL, QUERY_HEADS, HEAD_SIZE)
    base_k = jax.random.normal(jax.random.fold_in(key, 11), shape_k, jnp.float32)
    base_q = jax.random.normal(jax.random.fold_in(key, 12), shape_q, jnp.float32)
    base_k = jnp.clip(base_k, -4.0, 4.0)
    base_q = jnp.clip(base_q, -4.0, 4.0)
    return (base_q, base_k)


def draw_rotated_queries(key, part):
    base_q, base_k = paired_states(key)
    return base_q.reshape(TOKEN_TOTAL, QUERY_HEADS * HEAD_SIZE).astype(jnp.bfloat16)


def draw_rotated_keys(key, part):
    base_q, base_k = paired_states(key)
    return base_k.reshape(TOKEN_TOTAL, KVH * HEAD_SIZE).astype(jnp.bfloat16)


def steps_of(rng, shape, split, low, largest):
    def one(dim, shards_of):
        heights = jax.random.uniform(jax.random.fold_in(jax.random.fold_in(rng, 6), dim), (shards_of,), jnp.float32, low / len(split), largest / len(split))
        return jnp.repeat(jnp.exp(heights), shape[dim] // shards_of).reshape((-1,) + (1,) * (len(shape) - dim - 1))

    factor_of = one(*split[0])
    for cut in split[1:]:
        factor_of = factor_of * one(*cut)
    return factor_of


def shared_out(stream_key, own, number, rows, amount, top, bound, lean):
    ranking = jax.random.permutation(stream_key, amount)
    crowded, common = portions_of(amount, rows * top, bound, lean, True), portions_of(amount, rows * top, bound, lean, False)
    places = jnp.arange(amount)

    def named(tallies, rotation):
        used = int((tallies > 0).sum())
        fixed = max(1, used // 4)
        moved = fixed + (places - fixed + rotation * (used - fixed)) % max(1, amount - fixed)
        return jnp.zeros((amount,), jnp.int32).at[ranking[jnp.where(places < fixed, places, moved)]].set(jnp.asarray(tallies, jnp.int32))

    tallies = jnp.where(number % 4 == 0, named(crowded, number // 4), named(common, number - number // 4 - 1))
    mixed = jax.random.permutation(jax.random.fold_in(own, 3), amount)
    source_of, receiver = mixed[0:amount // 2 * 2:2], mixed[1:amount // 2 * 2:2]
    room = jnp.minimum(tallies[source_of] - 1, bound - tallies[receiver]) // 2
    room = jnp.where((source_of == ranking[0]) | (receiver == ranking[0]) | (tallies[receiver] == 0), 0, jnp.maximum(room, 0))
    moved = jax.random.randint(jax.random.fold_in(own, 4), (amount // 2,), 0, 1 << 20) % (room + 1)
    tallies = tallies.at[source_of].add(-moved).at[receiver].add(moved)
    members = jnp.searchsorted(jnp.cumsum(tallies), jnp.arange(rows * top), side="right").astype(jnp.int32)
    grid = members.reshape(top, rows).T
    grid = grid[jax.random.permutation(jax.random.fold_in(own, 1), rows)]
    rotation = jax.random.randint(jax.random.fold_in(own, 2), (rows, 1), 0, top)
    return jnp.take_along_axis(grid, (jnp.arange(top)[None, :] + rotation) % top, axis=1)


def portions_of(amount, total, reach, skew, full):
    weights = [(1 << 20) // math.isqrt(standing ** skew) + 1 for standing in range(1, amount + 1)]
    largest = reach if full else min(reach, max(-(-total // amount), total * weights[0] // sum(weights)))
    least = 1 if total - largest >= amount - 1 else 0
    holding, rest = [largest] + [least] * (amount - 1), total - largest - least * (amount - 1)
    while rest > 0:
        candidates = [i for i in range(1, amount) if holding[i] < largest] or [i for i in range(1, amount) if holding[i] < reach]
        pool, remaining = sum([weights[i] for i in candidates]), rest
        for i in candidates:
            more = min(reach - holding[i], max(1, remaining * weights[i] // pool), rest)
            holding[i] = holding[i] + more
            rest = rest - more
    return np.array(holding)


def normal_values(own_key, extent, spread, reach, shards=(), kind=jnp.bfloat16):
    level = steps_of(own_key, extent, shards, -0.22, 0.18) if shards else 1.0
    entries = jax.random.normal(own_key, extent, jnp.float32) * spread * level
    return jnp.minimum(jnp.maximum(entries, -reach), reach).astype(kind)


def setup_inputs(seed: int = 0) -> dict:
    streams_of = jax.random.split(jax.random.key(seed), 15)
    output_gradient = normal_values(streams_of[0], (TOKEN_TOTAL, MODEL_DIM), 1.0, 6.0, ((0, 32),))
    expert_choice_index_keys = jax.random.split(jax.random.fold_in(streams_of[1], 1), TOKEN_TOTAL // TOK_DEV)
    expert_choice_index_turns = jax.random.permutation(jax.random.fold_in(streams_of[1], 3), TOKEN_TOTAL // TOK_DEV)
    expert_choice_index = jax.vmap(lambda own, number: shared_out(jax.random.fold_in(streams_of[1], 2), own, number, TOK_DEV, EXPERT_COUNT, TOP, CAP, 2))(expert_choice_index_keys, expert_choice_index_turns).reshape((TOKEN_TOTAL, TOP))
    routing_weight = jnp.clip(0.05 + 0.25 * jax.random.uniform(streams_of[2], (TOKEN_TOTAL, TOP), jnp.float32) ** steps_of(streams_of[2], (TOKEN_TOTAL, TOP), ((0, 32),), -0.2, 0.2), 0.05, 0.3)
    stored_gate_preact = normal_values(streams_of[3], (EXPERT_COUNT, SLOTS, 2 * FFN_HIDDEN), 1.0, 6.0, ((0, 32),))
    gate_up_weight = normal_values(streams_of[4], (EXPERT_COUNT, MODEL_DIM, 2 * FFN_HIDDEN), MODEL_DIM ** -0.5, 0.125, ((0, 32),))
    down_weight = normal_values(streams_of[5], (EXPERT_COUNT, FFN_HIDDEN, MODEL_DIM), FFN_HIDDEN ** -0.5, 0.21875, ((0, 32),))
    down_first_factor = normal_values(streams_of[6], (EXPERT_COUNT, ADAPTER_RANK, FFN_HIDDEN), FFN_HIDDEN ** -0.5, 0.21875, ((0, 32),))
    down_second_factor = normal_values(streams_of[7], (EXPERT_COUNT, ADAPTER_RANK, MODEL_DIM), ADAPTER_RANK ** -0.5, 0.75, ((0, 32),))
    rotated_queries = draw_rotated_queries(jax.random.fold_in(streams_of[14], 71), 0)
    rotated_keys = draw_rotated_keys(jax.random.fold_in(streams_of[14], 71), 0)
    stored_values = normal_values(streams_of[10], (TOKEN_TOTAL, KVH * HEAD_SIZE), 1.0, 6.0, ((0, 4),))
    output_weight = normal_values(streams_of[11], (QUERY_HEADS * HEAD_SIZE, MODEL_DIM), (QUERY_HEADS * HEAD_SIZE) ** -0.5, 0.09375, ((0, 8),))
    output_first_factor = normal_values(streams_of[12], (ADAPTER_RANK, QUERY_HEADS * HEAD_SIZE), (QUERY_HEADS * HEAD_SIZE) ** -0.5, 0.09375, ((1, 8),))
    output_second_factor = normal_values(streams_of[13], (ADAPTER_RANK, MODEL_DIM), ADAPTER_RANK ** -0.5, 0.75)
    return dict(output_gradient=output_gradient, expert_choice_index=expert_choice_index, routing_weight=routing_weight, stored_gate_preact=stored_gate_preact, gate_up_weight=gate_up_weight, down_weight=down_weight, down_first_factor=down_first_factor, down_second_factor=down_second_factor, rotated_queries=rotated_queries, rotated_keys=rotated_keys, stored_values=stored_values, output_weight=output_weight, output_first_factor=output_first_factor, output_second_factor=output_second_factor)


adapter_scale = 2.0
neg_big = -1e30


def expert_backward(routed_rows, saved_rows, gate_up, down_output, lowrank_first, low_b):
    pre_gate = saved_rows[:, :FFN_HIDDEN].astype(jnp.float32)
    pre_up = saved_rows[:, FFN_HIDDEN:].astype(jnp.float32)
    sigmoid = jax.nn.sigmoid(pre_gate)
    activated = pre_gate * sigmoid
    slope = sigmoid * (1.0 + pre_gate * (1.0 - sigmoid))
    hidden_activity = (activated * pre_up).astype(jnp.bfloat16)
    lowrank_input = jnp.dot(hidden_activity, lowrank_first.T, preferred_element_type=jnp.float32).astype(jnp.bfloat16)
    lowrank_gradient = jnp.dot(routed_rows, low_b.T, preferred_element_type=jnp.float32).astype(jnp.bfloat16)
    gradient_second = adapter_scale * jnp.dot(lowrank_input.T, routed_rows, preferred_element_type=jnp.float32)
    gradient_first = adapter_scale * jnp.dot(lowrank_gradient.T, hidden_activity, preferred_element_type=jnp.float32)
    hidden_gradient = jnp.dot(routed_rows, down_output.T, preferred_element_type=jnp.float32) + adapter_scale * jnp.dot(lowrank_gradient, lowrank_first, preferred_element_type=jnp.float32)
    grad_pre = jnp.concatenate([hidden_gradient * pre_up * slope, hidden_gradient * activated], axis=1).astype(jnp.bfloat16)
    grad_rows = jnp.dot(grad_pre, gate_up.T, preferred_element_type=jnp.float32).astype(jnp.bfloat16)
    return grad_rows, gradient_first, gradient_second


def head_backward(query_rows, key_rows, value_rows, grad_rows):
    att_scale = HEAD_SIZE ** -0.5
    scores = jnp.dot(query_rows, key_rows.T, preferred_element_type=jnp.float32) * att_scale
    positions = jnp.arange(PIECE, dtype=jnp.int32)
    scores = jnp.where(positions[:, None] >= positions[None, :], scores, neg_big)
    probs_full = jnp.exp(scores - jnp.max(scores, axis=1, keepdims=True))
    probs_full = probs_full / jnp.sum(probs_full, axis=1, keepdims=True)
    probs_low = probs_full.astype(jnp.bfloat16)
    attended = jnp.dot(probs_low, value_rows, preferred_element_type=jnp.float32).astype(jnp.bfloat16)
    grad_probs = jnp.dot(grad_rows, value_rows.T, preferred_element_type=jnp.float32)
    row_delta = jnp.sum(grad_rows.astype(jnp.float32) * attended.astype(jnp.float32), axis=1, keepdims=True)
    grad_scores = (probs_full * (grad_probs - row_delta)).astype(jnp.bfloat16)
    grad_query = att_scale * jnp.dot(grad_scores, key_rows, preferred_element_type=jnp.float32)
    grad_key = att_scale * jnp.dot(grad_scores.T, query_rows, preferred_element_type=jnp.float32)
    grad_value = jnp.dot(probs_low.T, grad_rows, preferred_element_type=jnp.float32)
    return attended, grad_query, grad_key, grad_value


def reference(output_gradient, expert_choice_index, routing_weight, stored_gate_preact, gate_up_weight, down_weight, down_first_factor, down_second_factor, rotated_queries, rotated_keys, stored_values, output_weight, output_first_factor, output_second_factor):
    block_count = TOKEN_TOTAL // TOK_DEV
    per_block = expert_choice_index.reshape(block_count, TOK_DEV * TOP)
    onehot = (per_block[:, :, None] == jnp.arange(EXPERT_COUNT, dtype=jnp.int32)[None, None, :]).astype(jnp.int32)
    before = jnp.cumsum(onehot, axis=1) - onehot
    slot_rank = jnp.sum(before * onehot, axis=2)
    source = jnp.arange(block_count, dtype=jnp.int32)[:, None]
    cells = (source * CAP + slot_rank).reshape(-1).astype(jnp.int32)
    gathered_owner = jnp.full((EXPERT_COUNT, SLOTS), -1, jnp.int32)
    gathered_owner = gathered_owner.at[expert_choice_index.reshape(-1), cells].set(jnp.arange(TOKEN_TOTAL * TOP, dtype=jnp.int32))
    flat_weights = routing_weight.reshape(-1)

    def expert_step(carry, packed):
        owners, saved_rows, gate_up, down_output, lowrank_first, low_b = packed
        live = owners >= 0
        safe_owner = jnp.maximum(owners, 0)
        token_rows = safe_owner // TOP
        weight = jnp.where(live, flat_weights[safe_owner], jnp.float32(0.0))
        routed_rows = (weight[:, None] * output_gradient[token_rows].astype(jnp.float32)).astype(jnp.bfloat16)
        grad_rows, gradient_first, gradient_second = expert_backward(routed_rows, saved_rows, gate_up, down_output, lowrank_first, low_b)
        contrib = jnp.where(live[:, None], grad_rows.astype(jnp.float32), jnp.float32(0.0))
        carry = carry.at[token_rows].add(contrib)
        return carry, (gradient_first, gradient_second)

    offset_prefix = jnp.zeros((TOKEN_TOTAL, MODEL_DIM), jnp.float32)
    merged_result, (first_factor_gradient, second_factor_gradient) = lax.scan(expert_step, offset_prefix, (gathered_owner, stored_gate_preact, gate_up_weight, down_weight, down_first_factor, down_second_factor))
    residual_gradient = (output_gradient.astype(jnp.float32) + merged_result).astype(jnp.bfloat16)

    lowrank_token = jnp.dot(residual_gradient, output_second_factor.T, preferred_element_type=jnp.float32).astype(jnp.bfloat16)
    head_gradient = (jnp.dot(residual_gradient, output_weight.T, preferred_element_type=jnp.float32) + adapter_scale * jnp.dot(lowrank_token, output_first_factor, preferred_element_type=jnp.float32)).astype(jnp.bfloat16)
    group_size = QUERY_HEADS // KVH

    def head_turn(number):
        piece_index = number // QUERY_HEADS
        head_index = number % QUERY_HEADS
        kv_index = head_index // group_size
        first_row = (piece_index * PIECE).astype(jnp.int32)
        query_rows = lax.dynamic_slice(rotated_queries, (first_row, (head_index * HEAD_SIZE).astype(jnp.int32)), (PIECE, HEAD_SIZE))
        grad_rows = lax.dynamic_slice(head_gradient, (first_row, (head_index * HEAD_SIZE).astype(jnp.int32)), (PIECE, HEAD_SIZE))
        key_rows = lax.dynamic_slice(rotated_keys, (first_row, (kv_index * HEAD_SIZE).astype(jnp.int32)), (PIECE, HEAD_SIZE))
        value_rows = lax.dynamic_slice(stored_values, (first_row, (kv_index * HEAD_SIZE).astype(jnp.int32)), (PIECE, HEAD_SIZE))
        return head_backward(query_rows, key_rows, value_rows, grad_rows)

    attended, grad_q, grad_k, grad_v = lax.map(head_turn, jnp.arange(N_GRP * QUERY_HEADS, dtype=jnp.int32))
    query_gradient = grad_q.reshape(N_GRP, QUERY_HEADS, PIECE, HEAD_SIZE).transpose(0, 2, 1, 3).reshape(TOKEN_TOTAL, QUERY_HEADS * HEAD_SIZE)
    key_gradient = grad_k.reshape(N_GRP, KVH, group_size, PIECE, HEAD_SIZE).sum(axis=2).transpose(0, 2, 1, 3).reshape(TOKEN_TOTAL, KVH * HEAD_SIZE)
    value_gradient = grad_v.reshape(N_GRP, KVH, group_size, PIECE, HEAD_SIZE).sum(axis=2).transpose(0, 2, 1, 3).reshape(TOKEN_TOTAL, KVH * HEAD_SIZE)
    attended_gathered = attended.reshape(N_GRP, QUERY_HEADS, PIECE, HEAD_SIZE).transpose(0, 2, 1, 3).reshape(TOKEN_TOTAL, QUERY_HEADS, HEAD_SIZE)
    output_first_gradient = adapter_scale * jnp.dot(lowrank_token.T, attended_gathered.reshape(TOKEN_TOTAL, QUERY_HEADS * HEAD_SIZE), preferred_element_type=jnp.float32)
    flattened = jnp.einsum('fxm,oxm->fxo', attended_gathered.astype(jnp.float32), output_first_factor.reshape(ADAPTER_RANK, QUERY_HEADS, HEAD_SIZE).astype(jnp.float32)).astype(jnp.bfloat16)
    output_second_gradient = adapter_scale * jnp.einsum('dfn,dj->nj', flattened.astype(jnp.float32), residual_gradient.astype(jnp.float32))
    return (first_factor_gradient, second_factor_gradient, residual_gradient, output_first_gradient, output_second_gradient, query_gradient, key_gradient, value_gradient)
```

```python
import functools

import jax
import jax.numpy as jnp
from jax import lax
from jax.experimental import pallas as pl
from jax.experimental.pallas import tpu as pltpu
from jax.sharding import PartitionSpec as P

QUERY_HEADS = 32
KVH = 4
HEAD_SIZE = 128

adapter_scale = 2.0
neg_big = -1e30
att_scale = HEAD_SIZE ** (-0.5)
VMEM_BYTES = 56 * 1024 * 1024


def contraction(left, right, left_dim, right_dim):
    return lax.dot_general(
        left, right, (((left_dim,), (right_dim,)), ((), ())), preferred_element_type=jnp.float32
    )


def across(value, step):
    count = lax.axis_size("dev")
    return lax.ppermute(value, "dev", [(i, i ^ step) for i in range(count)])


def shift(value, step):
    count = lax.axis_size("grp")
    return lax.ppermute(value, "grp", [(i, (i + step) % count) for i in range(count)])


def forward_kernel(place, q_ref, k_ref, v_ref, a_ref, probs_ref, att_ref, even_ref, odd_ref, folded):
    head = pl.program_id(0)
    rows = q_ref.shape[0]
    token_block = folded.shape[2]
    block = min(256, rows)

    @pl.when(head == 0)
    def _():
        folded[...] = jnp.zeros_like(folded)

    for first in range(0, rows, block):
        last = first + block
        scores = contraction(q_ref[first:last, :], k_ref[:last, :], 1, 1) * att_scale
        row = first + lax.broadcasted_iota(jnp.int32, scores.shape, 0)
        column = lax.broadcasted_iota(jnp.int32, scores.shape, 1)
        scores = jnp.where(row >= column, scores, neg_big)
        weights = jnp.exp(scores - jnp.max(scores, axis=1, keepdims=True))
        weights = weights * (1.0 / jnp.sum(weights, axis=1, keepdims=True))
        low = weights.astype(jnp.bfloat16)
        probs_ref[0, first:last, :last] = low
        attended = jnp.dot(low, v_ref[:last, :], preferred_element_type=jnp.float32).astype(
            jnp.bfloat16
        )
        att_ref[first:last, :] = attended
        part = contraction(a_ref[...], attended, 1, 1).astype(jnp.bfloat16).astype(jnp.float32)
        for inner in range(0, block, token_block):
            number = (first + inner) // token_block
            folded[number] = folded[number] + part[:, inner : inner + token_block]

    @pl.when(head == pl.num_programs(0) - 1)
    def _():
        for j in range(even_ref.shape[0]):
            even_ref[j] = folded[place[0] ^ (2 * j)].astype(even_ref.dtype)
            odd_ref[j] = folded[place[0] ^ (2 * j + 1)].astype(odd_ref.dtype)


def attention_forward(place, queries, keys, values, first_factor, token_block):
    rows, width = queries.shape
    heads = width // HEAD_SIZE
    rank = first_factor.shape[0]
    pairs = rows // token_block // 2
    of_head = pl.BlockSpec((rows, HEAD_SIZE), lambda h, place: (0, h))
    of_group = pl.BlockSpec((rows, HEAD_SIZE), lambda h, place: (0, place[1]))
    part = pl.BlockSpec((pairs, rank, token_block), lambda h, place: (0, 0, 0))
    part_shape = jax.ShapeDtypeStruct((pairs, rank, token_block), jnp.bfloat16)
    return pl.pallas_call(
        forward_kernel,
        grid_spec=pltpu.PrefetchScalarGridSpec(
            num_scalar_prefetch=1,
            grid=(heads,),
            in_specs=[
                of_head,
                of_group,
                of_group,
                pl.BlockSpec((rank, HEAD_SIZE), lambda h, place: (0, h)),
            ],
            out_specs=[
                pl.BlockSpec((1, rows, rows), lambda h, place: (h, 0, 0)),
                of_head,
                part,
                part,
            ],
            scratch_shapes=[pltpu.VMEM((2 * pairs, rank, token_block), jnp.float32)],
        ),
        out_shape=[
            jax.ShapeDtypeStruct((heads, rows, rows), jnp.bfloat16),
            jax.ShapeDtypeStruct((rows, width), jnp.bfloat16),
            part_shape,
            part_shape,
        ],
        compiler_params=pltpu.CompilerParams(
            dimension_semantics=("arbitrary",), vmem_limit_bytes=VMEM_BYTES
        ),
        name="attention_forward",
    )(place, queries, keys, values, first_factor)


def head_kernel(place, *refs):
    count = len(refs) - 5
    blocks = refs[:count]
    weight_ref, first_ref, second_ref, grad_ref, low_ref = refs[count:]
    rows = blocks[0].shape[0]
    pairs = count // 2
    for j in range(pairs):
        gradient = jnp.concatenate([blocks[j][...], blocks[pairs + j][...]], axis=0)
        low = contraction(gradient, second_ref[...], 1, 1).astype(jnp.bfloat16)
        result = contraction(gradient, weight_ref[...], 1, 1)
        result = result + adapter_scale * jnp.dot(
            low, first_ref[...], preferred_element_type=jnp.float32
        )
        result = result.astype(jnp.bfloat16)
        for half in range(2):
            at = pl.ds(pl.multiple_of((place[0] ^ (2 * j + half)) * rows, rows), rows)
            grad_ref[at, :] = result[half * rows : (half + 1) * rows]
            low_ref[at, :] = low[half * rows : (half + 1) * rows]


def head_gradients(place, blocks, weight, first_factor, second_factor):
    rows = blocks[0].shape[0] * len(blocks)
    whole = lambda a: pl.BlockSpec(a.shape, lambda i, place: (0,) * a.ndim)
    operands = [*blocks, weight, first_factor, second_factor]
    outs = [
        jax.ShapeDtypeStruct((rows, weight.shape[0]), jnp.bfloat16),
        jax.ShapeDtypeStruct((rows, second_factor.shape[0]), jnp.bfloat16),
    ]
    return pl.pallas_call(
        head_kernel,
        grid_spec=pltpu.PrefetchScalarGridSpec(
            num_scalar_prefetch=1,
            grid=(1,),
            in_specs=[whole(a) for a in operands],
            out_specs=[whole(a) for a in outs],
        ),
        out_shape=outs,
        compiler_params=pltpu.CompilerParams(
            dimension_semantics=("arbitrary",), vmem_limit_bytes=VMEM_BYTES
        ),
        name="head_gradients",
    )(place, *operands)


def backward_kernel(
    place, q_ref, k_ref, v_ref, g_ref, att_ref, probs_ref, dq_ref, even_ref, odd_ref, dk, dv
):
    head = pl.program_id(0)
    rows = q_ref.shape[0]
    block = min(256, rows)
    token_block = even_ref.shape[1]

    @pl.when(head == 0)
    def _():
        dk[...] = jnp.zeros_like(dk)
        dv[...] = jnp.zeros_like(dv)

    for first in range(0, rows, block):
        last = first + block
        gradient = g_ref[first:last, :]
        query = q_ref[first:last, :]
        probs = probs_ref[0, first:last, :last]
        grad_probs = contraction(gradient, v_ref[:last, :], 1, 1)
        delta = jnp.sum(
            gradient.astype(jnp.float32) * att_ref[first:last, :].astype(jnp.float32),
            axis=1,
            keepdims=True,
        )
        grad_scores = (probs.astype(jnp.float32) * (grad_probs - delta)).astype(jnp.bfloat16)
        dq_ref[first:last, :] = att_scale * jnp.dot(
            grad_scores, k_ref[:last, :], preferred_element_type=jnp.float32
        )
        dk[:last, :] += contraction(grad_scores, query, 0, 0)
        dv[:last, :] += contraction(probs, gradient, 0, 0)

    @pl.when(head == pl.num_programs(0) - 1)
    def _():
        for j in range(even_ref.shape[0]):
            for half, ref in enumerate((even_ref, odd_ref)):
                number = place[0] ^ (2 * j + half)
                at = pl.ds(pl.multiple_of(number * token_block, token_block), token_block)
                ref[j, :, :HEAD_SIZE] = (dk[at, :] * att_scale).astype(ref.dtype)
                ref[j, :, HEAD_SIZE:] = dv[at, :].astype(ref.dtype)


def attention_backward(place, queries, keys, values, gradient, attended, probs, token_block):
    rows, width = queries.shape
    heads = width // HEAD_SIZE
    pairs = rows // token_block // 2
    of_head = pl.BlockSpec((rows, HEAD_SIZE), lambda h, place: (0, h))
    of_group = pl.BlockSpec((rows, HEAD_SIZE), lambda h, place: (0, place[1]))
    part = pl.BlockSpec((pairs, token_block, 2 * HEAD_SIZE), lambda h, place: (0, 0, 0))
    part_shape = (pairs, token_block, 2 * HEAD_SIZE)
    return pl.pallas_call(
        backward_kernel,
        grid_spec=pltpu.PrefetchScalarGridSpec(
            num_scalar_prefetch=1,
            grid=(heads,),
            in_specs=[
                of_head,
                of_group,
                of_group,
                of_head,
                of_head,
                pl.BlockSpec((1, rows, rows), lambda h, place: (h, 0, 0)),
            ],
            out_specs=[of_head, part, part],
            scratch_shapes=[
                pltpu.VMEM((rows, HEAD_SIZE), jnp.float32),
                pltpu.VMEM((rows, HEAD_SIZE), jnp.float32),
            ],
        ),
        out_shape=[
            jax.ShapeDtypeStruct((rows, width), jnp.float32),
            jax.ShapeDtypeStruct(part_shape, jnp.float32),
            jax.ShapeDtypeStruct(part_shape, jnp.bfloat16),
        ],
        compiler_params=pltpu.CompilerParams(
            dimension_semantics=("arbitrary",), vmem_limit_bytes=VMEM_BYTES
        ),
        name="attention_backward",
    )(place, queries, keys, values, gradient, attended, probs)


def planes_sum(parts, grp_index):
    count = len(parts)
    total = None
    for plane in range(count):
        term = parts[0].astype(jnp.float32)
        for step in range(1, count):
            here = (grp_index - step) % count == plane
            term = jnp.where(here, parts[step].astype(jnp.float32), term)
        total = term if total is None else total + term
    return total


def on_device(
    output_gradient,
    expert_choice_index,
    routing_weight,
    stored_gate_preact,
    gate_up_weight,
    down_weight,
    down_first_factor,
    down_second_factor,
    rotated_queries,
    rotated_keys,
    stored_values,
    output_weight,
    output_first_factor,
    output_second_factor,
):
    tok_rows, model_width = output_gradient.shape
    grp_count = lax.axis_size("grp")
    dev_count = lax.axis_size("dev")
    pairs = dev_count // 2
    experts = grp_count * dev_count
    slot_count = stored_gate_preact.shape[1]
    capacity = slot_count // experts
    chunk = dev_count * capacity
    width_ff = down_weight.shape[1]
    grp_index = lax.axis_index("grp")
    dev_index = lax.axis_index("dev")
    device_share = rotated_queries.shape[1] // HEAD_SIZE
    piece_len = rotated_queries.shape[0]
    kv_index = dev_index * device_share // (QUERY_HEADS // KVH)
    place = jnp.stack([dev_index, kv_index]).astype(jnp.int32)

    order = [2 * j for j in range(pairs)] + [2 * j + 1 for j in range(pairs)]

    ordinal = jnp.arange(experts, dtype=jnp.int32)
    in_plane = ordinal % dev_count
    distance = jnp.where(in_plane < pairs, 2 * in_plane, 2 * (in_plane - pairs) + 1)
    expert_of = ((grp_index + ordinal // dev_count) % grp_count) * dev_count + (
        dev_index ^ distance
    )
    named = expert_choice_index.T[:, None, :] == expert_of[None, :, None]
    chosen = jnp.any(named, axis=0)
    weight_of = jnp.sum(jnp.where(named, routing_weight.T[:, None, :], 0.0), axis=0)
    token = jnp.arange(tok_rows, dtype=jnp.int32)
    earlier = (token[:, None] < token[None, :]).astype(jnp.bfloat16)
    rank_of = jnp.dot(
        chosen.astype(jnp.bfloat16), earlier, preferred_element_type=jnp.float32
    )
    table = jnp.stack([jnp.where(chosen, rank_of, -1.0), weight_of]).reshape(
        2, grp_count, dev_count, tok_rows
    )

    tokens_at = [output_gradient] + [shift(output_gradient, s) for s in range(1, grp_count)]
    tables_at = [table[:, 0]] + [shift(table[:, s], s) for s in range(1, grp_count)]

    line = jnp.arange(chunk, dtype=jnp.int32)
    source = line // capacity
    source_distance = jnp.where(source < pairs, 2 * source, 2 * (source - pairs) + 1)
    saved_line = (dev_index ^ source_distance) * capacity + line % capacity
    reorder = (saved_line[:, None] == line[None, :]).astype(jnp.bfloat16)

    slot = jnp.arange(capacity, dtype=jnp.float32)

    def placement(step):
        ranks, weights = tables_at[step]
        filled = ranks[:, None, :] == slot[None, :, None]
        row_weight = jnp.sum(jnp.where(filled, weights[:, None, :], 0.0), axis=2)
        return filled.astype(jnp.bfloat16), row_weight

    placements = [placement(s) for s in range(grp_count)]

    def message_rows(step, j):
        filled = placements[step][0]
        return jnp.concatenate([filled[j], filled[pairs + j]], axis=0)

    def dispatched(step):
        weights = placements[step][1]
        messages = []
        for j in range(pairs):
            scale = jnp.concatenate([weights[j], weights[pairs + j]])
            rows = jnp.dot(
                message_rows(step, j), tokens_at[step], preferred_element_type=jnp.float32
            )
            messages.append((rows * scale[:, None]).astype(jnp.bfloat16))
        got = [messages[0]] + [across(messages[j], 2 * j) for j in range(1, pairs)]
        passed = across(jnp.concatenate([part[capacity:] for part in got], axis=0), 1)
        return jnp.concatenate([part[:capacity] for part in got] + [passed], axis=0)

    first_factor = down_first_factor[0]
    second_factor = down_second_factor[0]

    def saved_of(step):
        plane = (grp_index - step) % grp_count
        rows = lax.dynamic_slice_in_dim(stored_gate_preact[0], plane * chunk, chunk, 0)
        rows = jnp.dot(reorder, rows, preferred_element_type=jnp.float32).astype(jnp.bfloat16)
        gate = rows[:, :width_ff].astype(jnp.float32)
        hidden = (gate * jax.nn.sigmoid(gate) * rows[:, width_ff:].astype(jnp.float32)).astype(
            jnp.bfloat16
        )
        return rows, hidden, contraction(hidden, first_factor, 1, 1).astype(jnp.bfloat16)

    saved = [saved_of(s) for s in range(grp_count)]

    probs, attended, fold_even, fold_odd = attention_forward(
        place, rotated_queries, rotated_keys, stored_values, output_first_factor, tok_rows
    )

    def plane_scatter(even, odd):
        both = (even.astype(jnp.float32) + across(odd, 1).astype(jnp.float32)).astype(
            jnp.bfloat16
        )
        return [both[0]] + [across(both[j], 2 * j) for j in range(1, pairs)]

    folded = sum(part.astype(jnp.float32) for part in plane_scatter(fold_even, fold_odd)).astype(
        jnp.bfloat16
    )

    routed = [dispatched(s) for s in range(grp_count)]

    grad_first = jnp.zeros(first_factor.shape, jnp.float32)
    grad_second = jnp.zeros(second_factor.shape, jnp.float32)

    def returned(step):
        rows, hidden, low_in = saved[step]
        gate = rows[:, :width_ff].astype(jnp.float32)
        up = rows[:, width_ff:].astype(jnp.float32)
        sigmoid = jax.nn.sigmoid(gate)
        slope = sigmoid * (1.0 + gate * (1.0 - sigmoid))
        low_grad = contraction(routed[step], second_factor, 1, 1).astype(jnp.bfloat16)
        grad_hidden = contraction(
            routed[step], down_weight[0], 1, 1
        ) + adapter_scale * jnp.dot(low_grad, first_factor, preferred_element_type=jnp.float32)
        grad_pre = jnp.concatenate(
            [grad_hidden * up * slope, grad_hidden * (gate * sigmoid)], axis=1
        ).astype(jnp.bfloat16)
        half = pairs * capacity
        odd = contraction(grad_pre[half:], gate_up_weight[0], 1, 1).astype(jnp.bfloat16)
        even = contraction(grad_pre[:half], gate_up_weight[0], 1, 1).astype(jnp.bfloat16)
        passed = across(odd, 1)
        parts = []
        for j in range(pairs):
            here = slice(j * capacity, (j + 1) * capacity)
            message = jnp.concatenate([even[here], passed[here]], axis=0)
            parts.append(message if j == 0 else across(message, 2 * j))
        rows_in = jnp.concatenate(parts, axis=0)
        spread = jnp.concatenate([message_rows(step, j) for j in range(pairs)], axis=0)
        total = contraction(spread, rows_in, 0, 0)
        first = contraction(low_grad, hidden, 0, 0)
        second = contraction(low_in, routed[step], 0, 0)
        if step:
            total = shift(total.astype(jnp.bfloat16), -step).astype(jnp.float32)
        return total, first, second

    steps = list(range(1, grp_count)) + [0]
    merged = output_gradient.astype(jnp.float32)
    for step in steps:
        total, first, second = returned(step)
        merged = merged + total
        grad_first = grad_first + first
        grad_second = grad_second + second
    residual = merged.astype(jnp.bfloat16)

    near = [residual] + [across(residual, 2 * j) for j in range(1, pairs)]
    blocks = near + [across(part, 1) for part in near]
    head_gradient, low_tokens = head_gradients(
        place, blocks, output_weight, output_first_factor, output_second_factor
    )

    column_term = adapter_scale * jnp.dot(folded, residual, preferred_element_type=jnp.float32)
    share = model_width // dev_count
    pieces = [
        lax.dynamic_slice_in_dim(column_term, (dev_index ^ k) * share, share, 1) for k in order
    ]
    even = jnp.stack(pieces[:pairs])
    odd = jnp.stack(pieces[pairs:]).astype(jnp.bfloat16)
    own = sum(part.astype(jnp.float32) for part in plane_scatter(even, odd))
    own = planes_sum([own] + [shift(own, s) for s in range(1, grp_count)], grp_index)
    output_second_gradient = lax.all_gather(own, "dev", axis=1, tiled=True)

    row_term = (adapter_scale * contraction(low_tokens, attended, 0, 0)).astype(jnp.bfloat16)
    output_first_gradient = planes_sum(
        [row_term] + [shift(row_term, s) for s in range(1, grp_count)], grp_index
    )

    query_gradient, pair_even, pair_odd = attention_backward(
        place,
        rotated_queries,
        rotated_keys,
        stored_values,
        head_gradient,
        attended,
        probs,
        tok_rows,
    )
    arrived = plane_scatter(pair_even, pair_odd)
    grads = []
    for group in range(KVH):
        grad = jnp.zeros(arrived[0].shape, jnp.float32)
        for j in range(pairs):
            of_part = (dev_index ^ (2 * j)) * device_share // (QUERY_HEADS // KVH)
            grad = grad + jnp.where(of_part == group, arrived[j].astype(jnp.float32), 0.0)
        grads.append(grad)
    key_gradient = jnp.concatenate([grad[:, :HEAD_SIZE] for grad in grads], axis=1)
    value_gradient = jnp.concatenate([grad[:, HEAD_SIZE:] for grad in grads], axis=1)
    return (
        adapter_scale * grad_first[None],
        adapter_scale * grad_second[None],
        residual,
        output_first_gradient,
        output_second_gradient,
        query_gradient,
        key_gradient,
        value_gradient,
    )


def solution(mesh):
    in_specs = (
        P(("grp", "dev"), None),
        P(("grp", "dev"), None),
        P(("grp", "dev"), None),
        P(("grp", "dev"), None, None),
        P(("grp", "dev"), None, None),
        P(("grp", "dev"), None, None),
        P(("grp", "dev"), None, None),
        P(("grp", "dev"), None, None),
        P("grp", "dev"),
        P("grp", None),
        P("grp", None),
        P("dev", None),
        P(None, "dev"),
        P(),
    )
    out_specs = (
        P(("grp", "dev"), None, None),
        P(("grp", "dev"), None, None),
        P(("grp", "dev"), None),
        P(None, "dev"),
        P(),
        P("grp", "dev"),
        P(("grp", "dev"), None),
        P(("grp", "dev"), None),
    )
    return jax.shard_map(
        on_device, mesh=mesh, in_specs=in_specs, out_specs=out_specs, check_vma=False
    )
```

```python
import functools

import jax
import jax.numpy as jnp
from jax import lax
from jax.experimental import pallas as pl
from jax.experimental.pallas import tpu as pltpu
from jax.sharding import PartitionSpec as P

QUERY_HEADS = 32
KVH = 4
HEAD_SIZE = 128

adapter_scale = 2.0
neg_big = -1e30
att_scale = HEAD_SIZE ** (-0.5)
VMEM_BYTES = 56 * 1024 * 1024
COST_UNIT = 1000000


def contraction(left, right, left_dim, right_dim):
    return lax.dot_general(
        left, right, (((left_dim,), (right_dim,)), ((), ())), preferred_element_type=jnp.float32
    )


def across(value, step):
    count = lax.axis_size("dev")
    return lax.ppermute(value, "dev", [(i, i ^ step) for i in range(count)])


def shift(value, step):
    count = lax.axis_size("grp")
    return lax.ppermute(value, "grp", [(i, (i + step) % count) for i in range(count)])


def unread(count):
    return [pl.BlockSpec(memory_space=pl.ANY)] * count


def estimate(cost):
    return pl.CostEstimate(flops=0, bytes_accessed=int(cost * COST_UNIT), transcendentals=0)


def whole_of(shape):
    return pl.BlockSpec(shape, lambda i, place: (0,) * len(shape))


def kernel_call(body, place, operands, specs, outs, out_specs, after, scratch=(), steps=1, name=None, cost=1.0):
    deps = len(after)

    def kernel(place_ref, *refs):
        count = len(operands)
        body(place_ref, *refs[:count], *refs[count + deps :])

    return pl.pallas_call(
        kernel,
        grid_spec=pltpu.PrefetchScalarGridSpec(
            num_scalar_prefetch=1,
            grid=(steps,),
            in_specs=[*specs, *unread(deps)],
            out_specs=out_specs,
            scratch_shapes=list(scratch),
        ),
        out_shape=outs,
        compiler_params=pltpu.CompilerParams(
            dimension_semantics=("arbitrary",), vmem_limit_bytes=VMEM_BYTES
        ),
        cost_estimate=estimate(cost),
        name=name,
    )(place, *operands, *after)


def bf16(*shape):
    return jax.ShapeDtypeStruct(shape, jnp.bfloat16)


def f32(*shape):
    return jax.ShapeDtypeStruct(shape, jnp.float32)


def filled_cells(ranks, count):
    cell = lax.broadcasted_iota(jnp.int32, (count, ranks.shape[1]), 0).astype(jnp.float32)
    return ranks == cell


def chip_part(place_ref, refs, j):
    return refs[0].at[(place_ref[0] // 2) ^ j] if len(refs) == 1 else refs[j]


def dispatch(place, own, other, tables, cells, stacked, after):
    planes = len(own)
    pairs = tables[0].shape[1]
    width = own[0].shape[1]

    def body(place_ref, *refs):
        for i in range(planes):
            own_ref, other_ref, table_ref = refs[i], refs[planes + i], refs[2 * planes + i]
            tokens = jnp.concatenate([own_ref[...], other_ref[...]], axis=0)
            for j in range(pairs):
                filled = filled_cells(table_ref[0, j : j + 1, :], cells)
                weight = jnp.sum(
                    jnp.where(filled, table_ref[1, j : j + 1, :], 0.0), axis=1, keepdims=True
                )
                rows = jnp.dot(
                    filled.astype(jnp.bfloat16), tokens, preferred_element_type=jnp.float32
                )
                out = chip_part(place_ref, refs[3 * planes :], j)
                out[i * cells : (i + 1) * cells, :] = (rows * weight).astype(jnp.bfloat16)

    operands = [*own, *other, *tables]
    outs = [bf16(planes * cells, width)] * pairs
    if stacked:
        outs = [bf16(pairs, planes * cells, width)]
    return kernel_call(
        body,
        place,
        operands,
        [whole_of(a.shape) for a in operands],
        outs,
        [whole_of(a.shape) for a in outs],
        after,
        name="dispatch",
        cost=3.5,
    )


def combine(place, messages, tables, token_block, after):
    planes = len(tables)
    pairs, both = tables[0].shape[1:]
    cells, width = messages[0].shape[-2] // planes, messages[0].shape[-1]
    count = len(messages)

    def body(place_ref, *refs):
        for i in range(planes):
            table_ref = refs[count + i]
            own_ref, other_ref = refs[count + planes + 2 * i : count + planes + 2 * i + 2]
            total = None
            for j in range(pairs):
                filled = filled_cells(table_ref[0, j : j + 1, :], cells).astype(jnp.bfloat16)
                rows = chip_part(place_ref, refs[:count], j)[i * cells : (i + 1) * cells, :]
                part = contraction(filled, rows, 0, 0)
                total = part if total is None else total + part
            own_ref[...] = total[:token_block]
            other_ref[...] = total[token_block:].astype(jnp.bfloat16)

    operands = [*messages, *tables]
    outs = [f32(token_block, width), bf16(both - token_block, width)] * planes
    result = kernel_call(
        body,
        place,
        operands,
        [whole_of(a.shape) for a in operands],
        outs,
        [whole_of(a.shape) for a in outs],
        after,
        name="combine",
        cost=4.5,
    )
    return result[::2], result[1::2]


def expert(
    place, steps, parts, saved, reorder, down, gate_up, first, second, cells, pairs, outs, after
):
    planes = len(steps)
    chunk = cells * pairs
    rows = planes * chunk
    width_ff, width = down.shape
    rank = first.shape[0]
    span = 256
    blocks = width_ff // span
    sides = 2
    columns = width // sides
    count, results = len(parts), len(outs)
    split_in = count > 1 or parts[0].ndim == 3
    split_out = results > 1 or len(outs[0].shape) == 3

    def body(place_ref, *refs):
        rows_in = refs[:count]
        reorder_ref = refs[count]
        gates = refs[count + 1 : count + 1 + planes]
        ups = refs[count + 1 + planes : count + 1 + 2 * planes]
        down_ref, back_ref, first_ref, second_ref = refs[count + 1 + 2 * planes :][:4]
        rest = refs[count + 5 + 2 * planes :]
        rows_out, (grad_first_ref, grad_second_ref) = rest[:results], rest[results : results + 2]
        routed, low_grad, low_in, grad_pre = rest[results + 2 :]
        number = pl.program_id(0)

        @pl.when(number == 0)
        def _():
            if split_in:
                for i in range(planes):
                    for j in range(pairs):
                        at = i * chunk + j * cells
                        part = chip_part(place_ref, rows_in, j)
                        routed[at : at + cells, :] = part[i * cells : (i + 1) * cells, :]
            else:
                routed[...] = rows_in[0][...]
            low_grad[...] = contraction(routed[...], second_ref[...], 1, 1).astype(jnp.bfloat16)
            low_in[...] = jnp.zeros_like(low_in)

        for block in range(blocks):

            @pl.when(number == block)
            def _():
                order = reorder_ref[...]
                gate = [
                    jnp.dot(order, ref[...], preferred_element_type=jnp.float32) for ref in gates
                ]
                up = [jnp.dot(order, ref[...], preferred_element_type=jnp.float32) for ref in ups]
                gate = jnp.concatenate(gate, axis=0) if planes > 1 else gate[0]
                up = jnp.concatenate(up, axis=0) if planes > 1 else up[0]
                sigmoid = jax.nn.sigmoid(gate)
                active = gate * sigmoid
                slope = sigmoid * (1.0 + gate * (1.0 - sigmoid))
                hidden = (active * up).astype(jnp.bfloat16)
                low_in[...] += contraction(hidden, first_ref[...], 1, 1)
                grad_first_ref[...] = adapter_scale * contraction(low_grad[...], hidden, 0, 0)
                grad_hidden = contraction(
                    routed[...], down_ref[...], 1, 1
                ) + adapter_scale * jnp.dot(
                    low_grad[...], first_ref[...], preferred_element_type=jnp.float32
                )
                at = block * span
                grad_pre[:, at : at + span] = (grad_hidden * up * slope).astype(jnp.bfloat16)
                grad_pre[:, width_ff + at : width_ff + at + span] = (grad_hidden * active).astype(
                    jnp.bfloat16
                )

        for side in range(sides):

            @pl.when(number == blocks + side)
            def _():
                result = contraction(grad_pre[...], back_ref[...], 1, 1).astype(jnp.bfloat16)
                if split_out:
                    for i in range(planes):
                        for j in range(pairs):
                            at = i * chunk + j * cells
                            part = chip_part(place_ref, rows_out, j)
                            part[i * cells : (i + 1) * cells, :] = result[at : at + cells]
                else:
                    rows_out[0][...] = result
                grad_second_ref[...] = adapter_scale * contraction(
                    low_in[...].astype(jnp.bfloat16),
                    routed[:, side * columns : (side + 1) * columns],
                    0,
                    0,
                )

    def inner(i):
        return jnp.minimum(i, blocks - 1)

    def outer(i):
        return jnp.maximum(i - blocks, 0)

    def saved_block(step, offset):
        return pl.BlockSpec(
            (chunk, span), lambda i, place: (place[2 + step], offset + inner(i))
        )

    specs = [
        *[whole_of(a.shape) for a in parts],
        whole_of(reorder.shape),
        *[saved_block(step, 0) for step in steps],
        *[saved_block(step, blocks) for step in steps],
        pl.BlockSpec((span, width), lambda i, place: (inner(i), 0)),
        pl.BlockSpec((columns, 2 * width_ff), lambda i, place: (outer(i), 0)),
        pl.BlockSpec((rank, span), lambda i, place: (0, inner(i))),
        whole_of(second.shape),
    ]
    result = kernel_call(
        body,
        place,
        [*parts, reorder, *[saved] * (2 * planes), down, gate_up, first, second],
        specs,
        [*outs, f32(rank, width_ff), f32(rank, width)],
        [
            *[
                pl.BlockSpec(
                    (*a.shape[:-1], columns),
                    lambda i, place, lead=(0,) * (len(a.shape) - 1): (*lead, outer(i)),
                )
                for a in outs
            ],
            pl.BlockSpec((rank, span), lambda i, place: (0, inner(i))),
            pl.BlockSpec((rank, columns), lambda i, place: (0, outer(i))),
        ],
        after,
        scratch=[
            pltpu.VMEM((rows, width), jnp.bfloat16),
            pltpu.VMEM((rows, rank), jnp.bfloat16),
            pltpu.VMEM((rows, rank), jnp.float32),
            pltpu.VMEM((rows, 2 * width_ff), jnp.bfloat16),
        ],
        steps=blocks + sides,
        name="expert",
        cost=8.0 + 4.5 * planes,
    )
    return result[:results], result[results], result[results + 1]


def head_gradients(place, j, own, other, weight, first, second, attended, after):
    rows, width = own.shape
    heads_width = weight.shape[0]
    rank = first.shape[0]

    def body(place_ref, own_ref, other_ref, weight_ref, first_ref, second_ref, att_ref, grad_ref, term_ref):
        gradient = jnp.concatenate([own_ref[...], other_ref[...]], axis=0)
        low = contraction(gradient, second_ref[...], 1, 1).astype(jnp.bfloat16)
        result = contraction(gradient, weight_ref[...], 1, 1)
        result = result + adapter_scale * jnp.dot(
            low, first_ref[...], preferred_element_type=jnp.float32
        )
        grad_ref[...] = result.astype(jnp.bfloat16)
        core = place_ref[0] % 2
        term = None
        for half in range(2):
            at = pl.ds(pl.multiple_of((core ^ half) * rows, rows), rows)
            part = contraction(low[half * rows : (half + 1) * rows], att_ref[at, :], 0, 0)
            term = part if term is None else term + part
        term_ref[...] = adapter_scale * term

    operands = [own, other, weight, first, second, attended]
    specs = [whole_of(a.shape) for a in operands[:5]] + [
        pl.BlockSpec((2 * rows, heads_width), lambda i, place: ((place[0] // 2) ^ j, 0))
    ]
    outs = [bf16(2 * rows, heads_width), f32(rank, heads_width)]
    return kernel_call(
        body, place, operands, specs, outs, [whole_of(a.shape) for a in outs], after, name="head_gradients", cost=4.7
    )


def forward_kernel(place, q_ref, k_ref, v_ref, a_ref, *refs):
    probs_ref, att_ref, folded = refs[-3:]
    head = pl.program_id(0)
    rows = q_ref.shape[0]
    token_block = folded.shape[2]
    block = min(256, rows)

    @pl.when(head == 0)
    def _():
        folded[...] = jnp.zeros_like(folded)

    for first in range(0, rows, block):
        last = first + block
        scores = contraction(q_ref[first:last, :], k_ref[:last, :], 1, 1) * att_scale
        row = first + lax.broadcasted_iota(jnp.int32, scores.shape, 0)
        column = lax.broadcasted_iota(jnp.int32, scores.shape, 1)
        scores = jnp.where(row >= column, scores, neg_big)
        weights = jnp.exp(scores - jnp.max(scores, axis=1, keepdims=True))
        weights = weights * (1.0 / jnp.sum(weights, axis=1, keepdims=True))
        low = weights.astype(jnp.bfloat16)
        probs_ref[0, first:last, :last] = low
        attended = jnp.dot(low, v_ref[:last, :], preferred_element_type=jnp.float32).astype(
            jnp.bfloat16
        )
        att_ref[first:last, :] = attended
        part = contraction(a_ref[...], attended, 1, 1).astype(jnp.bfloat16).astype(jnp.float32)
        for inner in range(0, block, token_block):
            number = (first + inner) // token_block
            folded[number] = folded[number] + part[:, inner : inner + token_block]


def attention_forward(place, queries, keys, values, first_factor, token_block, span, earlier, after):
    rows, width = queries.shape
    heads = width // HEAD_SIZE
    rank = first_factor.shape[0]
    start, count = span
    of_head = pl.BlockSpec((rows, HEAD_SIZE), lambda h, place: (0, start + h))
    of_group = pl.BlockSpec((rows, HEAD_SIZE), lambda h, place: (0, place[1]))
    part = (rows // token_block, rank, token_block)
    return pl.pallas_call(
        forward_kernel,
        grid_spec=pltpu.PrefetchScalarGridSpec(
            num_scalar_prefetch=1,
            grid=(count,),
            in_specs=[
                of_head,
                of_group,
                of_group,
                pl.BlockSpec((rank, HEAD_SIZE), lambda h, place: (0, start + h)),
                *unread(len(earlier) + len(after)),
            ],
            out_specs=[
                pl.BlockSpec((1, rows, rows), lambda h, place: (start + h, 0, 0)),
                of_head,
                pl.BlockSpec(part, lambda h, place: (0, 0, 0)),
            ],
        ),
        out_shape=[
            bf16(heads, rows, rows),
            bf16(rows, width),
            f32(*part),
        ],
        input_output_aliases={5 + n: n for n in range(len(earlier))},
        compiler_params=pltpu.CompilerParams(
            dimension_semantics=("arbitrary",), vmem_limit_bytes=VMEM_BYTES
        ),
        cost_estimate=estimate(2.2 * rows / 512 * count),
        name="attention_forward",
    )(place, queries, keys, values, first_factor, *earlier, *after)


def backward_kernel(place, q_ref, k_ref, v_ref, att_ref, probs_ref, *refs):
    dq_ref, even_ref, odd_ref, dk, dv, g_ref = refs[-6:]
    head = pl.program_id(0)
    rows = q_ref.shape[0]
    block = min(256, rows)
    pairs, token_block = even_ref.shape[:2]
    for j in range(pairs):
        for half in range(2):
            number = place[0] ^ (2 * j + half)
            at = pl.ds(pl.multiple_of(number * token_block, token_block), token_block)
            g_ref[at, :] = refs[j][half * token_block : (half + 1) * token_block, :]

    @pl.when(head == 0)
    def _():
        dk[...] = jnp.zeros_like(dk)
        dv[...] = jnp.zeros_like(dv)

    for first in range(0, rows, block):
        last = first + block
        gradient = g_ref[first:last, :]
        query = q_ref[first:last, :]
        probs = probs_ref[0, first:last, :last]
        grad_probs = contraction(gradient, v_ref[:last, :], 1, 1)
        delta = jnp.sum(
            gradient.astype(jnp.float32) * att_ref[first:last, :].astype(jnp.float32),
            axis=1,
            keepdims=True,
        )
        grad_scores = (probs.astype(jnp.float32) * (grad_probs - delta)).astype(jnp.bfloat16)
        dq_ref[first:last, :] = att_scale * jnp.dot(
            grad_scores, k_ref[:last, :], preferred_element_type=jnp.float32
        )
        dk[:last, :] += contraction(grad_scores, query, 0, 0)
        dv[:last, :] += contraction(probs, gradient, 0, 0)

    @pl.when(head == pl.num_programs(0) - 1)
    def _():
        for j in range(even_ref.shape[0]):
            for half, ref in enumerate((even_ref, odd_ref)):
                number = place[0] ^ (2 * j + half)
                at = pl.ds(pl.multiple_of(number * token_block, token_block), token_block)
                ref[j, :, :HEAD_SIZE] = (dk[at, :] * att_scale).astype(ref.dtype)
                ref[j, :, HEAD_SIZE:] = dv[at, :].astype(ref.dtype)


def attention_backward(place, queries, keys, values, attended, probs, gradients, token_block, after):
    rows, width = queries.shape
    heads = width // HEAD_SIZE
    pairs = rows // token_block // 2
    of_head = pl.BlockSpec((rows, HEAD_SIZE), lambda h, place: (0, h))
    of_group = pl.BlockSpec((rows, HEAD_SIZE), lambda h, place: (0, place[1]))
    part = pl.BlockSpec((pairs, token_block, 2 * HEAD_SIZE), lambda h, place: (0, 0, 0))
    part_shape = (pairs, token_block, 2 * HEAD_SIZE)
    return pl.pallas_call(
        backward_kernel,
        grid_spec=pltpu.PrefetchScalarGridSpec(
            num_scalar_prefetch=1,
            grid=(heads,),
            in_specs=[
                of_head,
                of_group,
                of_group,
                of_head,
                pl.BlockSpec((1, rows, rows), lambda h, place: (h, 0, 0)),
                *[pl.BlockSpec((2 * token_block, HEAD_SIZE), lambda h, place: (0, h))] * pairs,
                *unread(len(after)),
            ],
            out_specs=[of_head, part, part],
            scratch_shapes=[
                pltpu.VMEM((rows, HEAD_SIZE), jnp.float32),
                pltpu.VMEM((rows, HEAD_SIZE), jnp.float32),
                pltpu.VMEM((rows, HEAD_SIZE), jnp.bfloat16),
            ],
        ),
        out_shape=[
            jax.ShapeDtypeStruct((rows, width), jnp.float32),
            jax.ShapeDtypeStruct(part_shape, jnp.float32),
            jax.ShapeDtypeStruct(part_shape, jnp.bfloat16),
        ],
        compiler_params=pltpu.CompilerParams(
            dimension_semantics=("arbitrary",), vmem_limit_bytes=VMEM_BYTES
        ),
        cost_estimate=estimate(11.8),
        name="attention_backward",
    )(place, queries, keys, values, attended, probs, *gradients, *after)


def planes_sum(parts, grp_index):
    count = len(parts)
    total = None
    for plane in range(count):
        term = parts[0].astype(jnp.float32)
        for step in range(1, count):
            here = (grp_index - step) % count == plane
            term = jnp.where(here, parts[step].astype(jnp.float32), term)
        total = term if total is None else total + term
    return total


def on_device(
    output_gradient,
    expert_choice_index,
    routing_weight,
    stored_gate_preact,
    gate_up_weight,
    down_weight,
    down_first_factor,
    down_second_factor,
    rotated_queries,
    rotated_keys,
    stored_values,
    output_weight,
    output_first_factor,
    output_second_factor,
):
    tok_rows, model_width = output_gradient.shape
    top_count = expert_choice_index.shape[1]
    grp_count = lax.axis_size("grp")
    dev_count = lax.axis_size("dev")
    pairs = dev_count // 2
    experts = grp_count * dev_count
    slot_count = stored_gate_preact.shape[1]
    capacity = slot_count // experts
    cells = 2 * capacity
    chunk = dev_count * capacity
    grp_index = lax.axis_index("grp")
    dev_index = lax.axis_index("dev")
    heads = rotated_queries.shape[1] // HEAD_SIZE
    group_size = QUERY_HEADS // KVH
    planes = (grp_index - jnp.arange(grp_count, dtype=jnp.int32)) % grp_count
    place = jnp.concatenate(
        [jnp.stack([dev_index, dev_index * heads // group_size]).astype(jnp.int32), planes]
    )

    ring = sorted(range(1, grp_count), key=lambda s: (min(s, grp_count - s), s))
    middle = (2 * len(ring) + 2) // 3
    groups = [g for g in ([0], ring[:middle], ring[middle:]) if g]

    choice = jnp.concatenate(
        [expert_choice_index.T.astype(jnp.float32), routing_weight.T], axis=0
    )
    tokens = {0: output_gradient}
    near_tokens = {0: across(output_gradient, 1)}
    choice = jnp.stack([choice, across(choice, 1)])

    token = jnp.arange(tok_rows, dtype=jnp.int32)
    earlier = (token[:, None] < token[None, :]).astype(jnp.bfloat16)
    plane_experts = (
        grp_index * dev_count + (dev_index ^ (2 * jnp.arange(pairs, dtype=jnp.int32)))
    ).astype(jnp.float32)

    def table_of(choice):
        ids, weights = choice[:, :top_count], choice[:, top_count:]
        named = ids[:, :, None, :] == plane_experts[None, None, :, None]
        chosen = jnp.any(named, axis=1)
        weight_of = jnp.sum(jnp.where(named, weights[:, :, None, :], 0.0), axis=1)
        rank_of = lax.dot_general(
            chosen.astype(jnp.bfloat16),
            earlier,
            (((2,), (0,)), ((), ())),
            preferred_element_type=jnp.float32,
        )
        first_cell = jnp.arange(2, dtype=jnp.float32)[:, None, None] * capacity
        ranks = jnp.where(chosen, rank_of + first_cell, -1.0)
        return jnp.stack(
            [
                jnp.concatenate([ranks[0], ranks[1]], axis=1),
                jnp.concatenate([weight_of[0], weight_of[1]], axis=1),
            ]
        )

    tables = {0: table_of(choice)}

    line = jnp.arange(chunk, dtype=jnp.int32)
    saved_line = (dev_index ^ (line // capacity)) * capacity + line % capacity
    reorder = (saved_line[:, None] == line[None, :]).astype(jnp.bfloat16)

    aligned = cells % 16 == 0
    last = []

    chips = [[2 * j + core for j in range(pairs)] for core in range(2)]

    def exchanged(parts):
        if len(parts) == 1:
            return [
                lax.all_to_all(parts[0], "dev", 0, 0, axis_index_groups=chips, tiled=True)
            ]
        return [parts[0]] + [across(parts[j], 2 * j) for j in range(1, pairs)]

    def dispatched(group, stacked):
        messages = dispatch(
            place,
            [tokens[s] for s in group],
            [near_tokens[s] for s in group],
            [tables[s] for s in group],
            cells,
            stacked and aligned,
            last,
        )
        last[:] = messages[:1]
        return exchanged(messages)

    def worked(group, parts, stacked):
        rows = len(group) * cells
        if not aligned:
            parts = [part.reshape(len(group), cells, model_width) for part in parts]
            parts = [jnp.concatenate(parts, axis=1).reshape(pairs * rows, model_width)]
            outs = [bf16(pairs * rows, model_width)]
        elif stacked:
            outs = [bf16(pairs, rows, model_width)]
        else:
            outs = [bf16(rows, model_width)] * pairs
        parts, first, second = expert(
            place,
            group,
            parts,
            stored_gate_preact[0],
            reorder,
            down_weight[0],
            gate_up_weight[0],
            down_first_factor[0],
            down_second_factor[0],
            cells,
            pairs,
            outs,
            last,
        )
        last[:] = [parts[0]]
        if not aligned:
            whole = parts[0].reshape(len(group), pairs, cells, model_width)
            parts = [whole[:, j].reshape(rows, model_width) for j in range(pairs)]
        return parts, first, second

    def combined(group, messages):
        owns, others = combine(place, messages, [tables[s] for s in group], tok_rows, last)
        last[:] = [others[0]]
        totals = []
        for s, own, other in zip(group, owns, others):
            total = own + across(other, 1).astype(jnp.float32)
            if s:
                total = shift(total.astype(jnp.bfloat16), -s).astype(jnp.float32)
            totals.append(total)
        return totals

    def forward(span, before):
        result = attention_forward(
            place,
            rotated_queries,
            rotated_keys,
            stored_values,
            output_first_factor,
            tok_rows,
            span,
            before,
            last,
        )
        last[:] = [result[2]]
        return result

    def sent_out(group, after):
        held = lax.optimization_barrier(((output_gradient, choice), after))[0]
        for s in group:
            choices[s] = shift(held[1], s)
        for s in group:
            tokens[s] = shift(held[0], s)

    def brought(group, after):
        held, _ = lax.optimization_barrier(
            ([tokens[s] for s in group], [choices[s] for s in group], last, after)
        )[:2], None
        for s, value, chosen in zip(group, *held):
            tokens[s] = value
            near_tokens[s] = across(value, 1)
            tables[s] = table_of(chosen)

    half = heads // 2
    choices, arrived, finished, back = {}, {}, {}, {}
    sent_out(groups[1], [])
    arrived[0] = dispatched(groups[0], True)
    probs, attended, folded_a = forward((0, half), [])
    brought(groups[1], [])
    if len(groups) > 2:
        sent_out(groups[2], [tokens[s] for s in groups[1]])
    arrived[1] = dispatched(groups[1], True)
    finished[0] = worked(groups[0], arrived[0], False)
    probs, attended, folded_b = forward((half, heads - half), [probs, attended])
    if len(groups) > 2:
        brought(groups[2], [])
        arrived[2] = dispatched(groups[2], True)
    for n in range(1, len(groups)):
        finished[n] = worked(groups[n], arrived[n], n == 2)
        back[n] = exchanged(finished[n][0])
    held, _ = lax.optimization_barrier((finished[0][0], last))
    back[0] = exchanged(held)
    totals = []
    for n in [*range(1, len(groups)), 0]:
        if n == 0:
            back[0], totals[: len(groups[1])] = lax.optimization_barrier(
                (back[0], totals[: len(groups[1])])
            )
        totals += combined(groups[n], back[n])
    folded, _ = lax.optimization_barrier(((folded_a + folded_b).astype(jnp.bfloat16), last))
    folded = lax.all_to_all(folded, "dev", 0, 0, tiled=True)
    folded = jnp.sum(folded.astype(jnp.float32), axis=0)
    grad_first = sum(finished[n][1] for n in finished)
    grad_second = sum(finished[n][2] for n in finished)
    residual = (output_gradient.astype(jnp.float32) + sum(totals)).astype(jnp.bfloat16)

    near = [residual] + [across(residual, 2 * j) for j in range(1, pairs)]
    grads, row_term = [], None
    for j in range(pairs):
        if j:
            near[j], _ = lax.optimization_barrier((near[j], last))
        grad, term = head_gradients(
            place,
            j,
            near[j],
            across(near[j], 1),
            output_weight,
            output_first_factor,
            output_second_factor,
            attended,
            last,
        )
        last[:] = [grad]
        grads.append(grad)
        row_term = term if row_term is None else row_term + term

    folded, _ = lax.optimization_barrier((folded.astype(jnp.bfloat16), grads[0]))
    column_term = (
        adapter_scale * jnp.dot(folded, residual, preferred_element_type=jnp.float32)
    ).astype(jnp.bfloat16)
    chip_term = (
        column_term.astype(jnp.float32) + across(column_term, 1).astype(jnp.float32)
    ).astype(jnp.bfloat16)
    share = model_width // pairs
    rank = column_term.shape[0]
    chip = dev_index // 2

    def columns(value, j):
        return lax.dynamic_slice_in_dim(value, (chip ^ j) * share, share, 1)

    mine = [columns(chip_term, 0)] + [
        across(columns(chip_term, j), 2 * j) for j in range(1, pairs)
    ]
    mine = sum(part.astype(jnp.float32) for part in mine).astype(jnp.bfloat16)

    row_term = row_term.astype(jnp.bfloat16)
    if row_term.shape == mine.shape:
        terms = jnp.concatenate([row_term, mine], axis=0)
        terms = planes_sum([terms] + [shift(terms, s) for s in range(1, grp_count)], grp_index)
        output_first_gradient, mine = terms[:rank], terms[rank:]
    else:
        output_first_gradient = planes_sum(
            [row_term] + [shift(row_term, s) for s in range(1, grp_count)], grp_index
        )
        mine = planes_sum([mine] + [shift(mine, s) for s in range(1, grp_count)], grp_index)
    mine = mine.astype(jnp.bfloat16)

    query_gradient, pair_even, pair_odd = attention_backward(
        place,
        rotated_queries,
        rotated_keys,
        stored_values,
        attended,
        probs,
        grads,
        tok_rows,
        last,
    )
    both = (pair_even + across(pair_odd, 1).astype(jnp.float32)).astype(jnp.bfloat16)
    lanes = both.shape[2]
    flat = mine.reshape(rank * share // lanes, lanes)
    ends = [jnp.concatenate([both[j], flat], axis=0) for j in range(pairs)]
    ends = [ends[0]] + [across(ends[j], 2 * j) for j in range(1, pairs)]
    grads = []
    for group in range(KVH):
        grad = jnp.zeros((tok_rows, lanes), jnp.float32)
        for j in range(pairs):
            here = (dev_index ^ (2 * j)) * heads // group_size == group
            grad = grad + jnp.where(here, ends[j][:tok_rows].astype(jnp.float32), 0.0)
        grads.append(grad)
    key_gradient = jnp.concatenate([grad[:, :HEAD_SIZE] for grad in grads], axis=1)
    value_gradient = jnp.concatenate([grad[:, HEAD_SIZE:] for grad in grads], axis=1)
    second_columns = []
    for number in range(pairs):
        part = jnp.zeros((rank, share), jnp.float32)
        for j in range(pairs):
            value = ends[j][tok_rows:].astype(jnp.float32).reshape(rank, share)
            part = part + jnp.where(chip ^ j == number, value, 0.0)
        second_columns.append(part)
    output_second_gradient = jnp.concatenate(second_columns, axis=1)
    return (
        grad_first[None],
        grad_second[None],
        residual,
        output_first_gradient,
        output_second_gradient,
        query_gradient,
        key_gradient,
        value_gradient,
    )


def solution(mesh):
    in_specs = (
        P(("grp", "dev"), None),
        P(("grp", "dev"), None),
        P(("grp", "dev"), None),
        P(("grp", "dev"), None, None),
        P(("grp", "dev"), None, None),
        P(("grp", "dev"), None, None),
        P(("grp", "dev"), None, None),
        P(("grp", "dev"), None, None),
        P("grp", "dev"),
        P("grp", None),
        P("grp", None),
        P("dev", None),
        P(None, "dev"),
        P(),
    )
    out_specs = (
        P(("grp", "dev"), None, None),
        P(("grp", "dev"), None, None),
        P(("grp", "dev"), None),
        P(None, "dev"),
        P(),
        P("grp", "dev"),
        P(("grp", "dev"), None),
        P(("grp", "dev"), None),
    )
    return jax.shard_map(
        on_device, mesh=mesh, in_specs=in_specs, out_specs=out_specs, check_vma=False
    )
```

```python
import functools

import jax
import jax.numpy as jnp
from jax import lax
from jax.experimental import pallas as pl
from jax.experimental.pallas import tpu as pltpu
from jax.sharding import PartitionSpec as P

QUERY_HEADS = 32
KVH = 4
HEAD_SIZE = 128

adapter_scale = 2.0
neg_big = -1e30
att_scale = HEAD_SIZE ** (-0.5)
VMEM_BYTES = 56 * 1024 * 1024
COST_UNIT = 1000000


def contraction(left, right, left_dim, right_dim):
    return lax.dot_general(
        left, right, (((left_dim,), (right_dim,)), ((), ())), preferred_element_type=jnp.float32
    )


def across(value, step):
    count = lax.axis_size("dev")
    return lax.ppermute(value, "dev", [(i, i ^ step) for i in range(count)])


def shift(value, step):
    count = lax.axis_size("grp")
    return lax.ppermute(value, "grp", [(i, (i + step) % count) for i in range(count)])


def unread(count):
    return [pl.BlockSpec(memory_space=pl.ANY)] * count


def estimate(cost):
    return pl.CostEstimate(flops=0, bytes_accessed=int(cost * COST_UNIT), transcendentals=0)


def whole_of(shape):
    return pl.BlockSpec(shape, lambda i, place: (0,) * len(shape))


def kernel_call(body, place, operands, specs, outs, out_specs, after, scratch=(), steps=1, name=None, cost=1.0):
    deps = len(after)

    def kernel(place_ref, *refs):
        count = len(operands)
        body(place_ref, *refs[:count], *refs[count + deps :])

    return pl.pallas_call(
        kernel,
        grid_spec=pltpu.PrefetchScalarGridSpec(
            num_scalar_prefetch=1,
            grid=(steps,),
            in_specs=[*specs, *unread(deps)],
            out_specs=out_specs,
            scratch_shapes=list(scratch),
        ),
        out_shape=outs,
        compiler_params=pltpu.CompilerParams(
            dimension_semantics=("arbitrary",), vmem_limit_bytes=VMEM_BYTES
        ),
        cost_estimate=estimate(cost),
        name=name,
    )(place, *operands, *after)


def bf16(*shape):
    return jax.ShapeDtypeStruct(shape, jnp.bfloat16)


def f32(*shape):
    return jax.ShapeDtypeStruct(shape, jnp.float32)


def filled_cells(ranks, count):
    cell = lax.broadcasted_iota(jnp.int32, (count, ranks.shape[1]), 0).astype(jnp.float32)
    return ranks == cell


def chip_part(place_ref, refs, j):
    return refs[0].at[(place_ref[0] // 2) ^ j] if len(refs) == 1 else refs[j]


def dispatch(place, own, other, tables, cells, stacked, extra, after):
    planes = len(own)
    pairs = tables[0].shape[1]
    width = own[0].shape[1]

    def body(place_ref, *refs):
        for i in range(planes):
            own_ref, other_ref, table_ref = refs[i], refs[planes + i], refs[2 * planes + i]
            tokens = jnp.concatenate([own_ref[...], other_ref[...]], axis=0)
            filled = [filled_cells(table_ref[0, j : j + 1, :], cells) for j in range(pairs)]
            weights = [
                jnp.sum(
                    jnp.where(filled[j], table_ref[1, j : j + 1, :], 0.0), axis=1, keepdims=True
                )
                for j in range(pairs)
            ]
            spread = jnp.concatenate([part.astype(jnp.bfloat16) for part in filled], axis=0)
            rows = jnp.dot(spread, tokens, preferred_element_type=jnp.float32)
            rows = (rows * jnp.concatenate(weights, axis=0)).astype(jnp.bfloat16)
            for j in range(pairs):
                out = chip_part(place_ref, refs[3 * planes + len(extra) :], j)
                out[i * cells : (i + 1) * cells, :] = rows[j * cells : (j + 1) * cells]

        if extra:
            parts = refs[3 * planes : 3 * planes + len(extra)]
            core = place_ref[0] % 2
            rank, lanes = extra[0].shape[1:]
            for chip in range(pairs):
                for half in range(2):
                    value = sum(ref[2 * chip + (core ^ half)] for ref in parts).astype(jnp.bfloat16)
                    for q in range(rank // added):
                        at = half * (width // 2) + q * lanes
                        refs[-1][chip, planes * cells :, at : at + lanes] = value[
                            q * added : (q + 1) * added
                        ]

    operands = [*own, *other, *tables, *extra]
    added = 2 * extra[0].shape[1] * extra[0].shape[2] // width if extra else 0
    outs = [bf16(planes * cells, width)] * pairs
    if stacked:
        outs = [bf16(pairs, planes * cells + added, width)]
    return kernel_call(
        body,
        place,
        operands,
        [whole_of(a.shape) for a in operands],
        outs,
        [whole_of(a.shape) for a in outs],
        after,
        name="dispatch",
        cost=3.5,
    )


def combine(place, messages, tables, token_block, after):
    planes = len(tables)
    pairs, both = tables[0].shape[1:]
    cells, width = messages[0].shape[-2] // planes, messages[0].shape[-1]
    count = len(messages)

    def body(place_ref, *refs):
        for i in range(planes):
            table_ref = refs[count + i]
            own_ref, other_ref = refs[count + planes + 2 * i : count + planes + 2 * i + 2]
            spread = jnp.concatenate(
                [
                    filled_cells(table_ref[0, j : j + 1, :], cells).astype(jnp.bfloat16)
                    for j in range(pairs)
                ],
                axis=0,
            )
            rows = [
                chip_part(place_ref, refs[:count], j)[i * cells : (i + 1) * cells, :]
                for j in range(pairs)
            ]
            total = contraction(spread, jnp.concatenate(rows, axis=0), 0, 0)
            own_ref[...] = total[:token_block]
            other_ref[...] = total[token_block:].astype(jnp.bfloat16)

    operands = [*messages, *tables]
    outs = [f32(token_block, width), bf16(both - token_block, width)] * planes
    result = kernel_call(
        body,
        place,
        operands,
        [whole_of(a.shape) for a in operands],
        outs,
        [whole_of(a.shape) for a in outs],
        after,
        name="combine",
        cost=4.5,
    )
    return result[::2], result[1::2]


def expert(place, steps, parts, saved, reorder, down, gate_up, first, second, cells, pairs, outs, after):
    planes = len(steps)
    chunk = cells * pairs
    rows = planes * chunk
    width_ff, width = down.shape
    rank = first.shape[0]
    span = 256
    blocks = width_ff // span
    sides = 2
    columns = width // sides
    count, results = len(parts), len(outs)
    split_in = count > 1 or parts[0].ndim == 3
    split_out = results > 1 or len(outs[0].shape) == 3

    def body(place_ref, *refs):
        rows_in = refs[:count]
        reorder_ref = refs[count]
        gates = refs[count + 1 : count + 1 + planes]
        ups = refs[count + 1 + planes : count + 1 + 2 * planes]
        down_ref, back_ref, first_ref, second_ref = refs[count + 1 + 2 * planes :][:4]
        rest = refs[count + 5 + 2 * planes :]
        rows_out, (hidden_ref, low_ref) = rest[:results], rest[results : results + 2]
        routed, low_grad, grad_pre, back, arrived = rest[results + 2 :]
        number = pl.program_id(0)

        def fetch(side):
            at = pl.ds(side * columns, columns)
            return pltpu.make_async_copy(back_ref.at[at, :], back.at[side], arrived.at[side])

        @pl.when(number == 0)
        def _():
            for side in range(sides):
                fetch(side).start()
            if split_in:
                for i in range(planes):
                    for j in range(pairs):
                        at = i * chunk + j * cells
                        part = chip_part(place_ref, rows_in, j)
                        routed[at : at + cells, :] = part[i * cells : (i + 1) * cells, :]
            else:
                routed[...] = rows_in[0][...]
            low = contraction(routed[...], second_ref[...], 1, 1).astype(jnp.bfloat16)
            low_grad[...] = low
            low_ref[...] = low

        for block in range(blocks):

            @pl.when(number == block)
            def _():
                order = reorder_ref[...]
                gate = [
                    jnp.dot(order, ref[...], preferred_element_type=jnp.float32) for ref in gates
                ]
                up = [jnp.dot(order, ref[...], preferred_element_type=jnp.float32) for ref in ups]
                gate = jnp.concatenate(gate, axis=0) if planes > 1 else gate[0]
                up = jnp.concatenate(up, axis=0) if planes > 1 else up[0]
                sigmoid = jax.nn.sigmoid(gate)
                active = gate * sigmoid
                slope = sigmoid * (1.0 + gate * (1.0 - sigmoid))
                hidden_ref[...] = (active * up).astype(jnp.bfloat16)
                grad_hidden = contraction(
                    routed[...], down_ref[...], 1, 1
                ) + adapter_scale * jnp.dot(
                    low_grad[...], first_ref[...], preferred_element_type=jnp.float32
                )
                at = block * span
                grad_pre[:, at : at + span] = (grad_hidden * up * slope).astype(jnp.bfloat16)
                grad_pre[:, width_ff + at : width_ff + at + span] = (grad_hidden * active).astype(
                    jnp.bfloat16
                )

        for side in range(sides):

            @pl.when(number == blocks + side)
            def _():
                fetch(side).wait()
                result = contraction(grad_pre[...], back[side], 1, 1).astype(jnp.bfloat16)
                if split_out:
                    for i in range(planes):
                        for j in range(pairs):
                            at = i * chunk + j * cells
                            part = chip_part(place_ref, rows_out, j)
                            part[i * cells : (i + 1) * cells, :] = result[at : at + cells]
                else:
                    rows_out[0][...] = result

    def inner(i):
        return jnp.minimum(i, blocks - 1)

    def outer(i):
        return jnp.maximum(i - blocks, 0)

    def saved_block(step, offset):
        return pl.BlockSpec(
            (chunk, span), lambda i, place: (place[2 + step], offset + inner(i))
        )

    specs = [
        *[whole_of(a.shape) for a in parts],
        whole_of(reorder.shape),
        *[saved_block(step, 0) for step in steps],
        *[saved_block(step, blocks) for step in steps],
        pl.BlockSpec((span, width), lambda i, place: (inner(i), 0)),
        pl.BlockSpec(memory_space=pl.ANY),
        pl.BlockSpec((rank, span), lambda i, place: (0, inner(i))),
        whole_of(second.shape),
    ]
    result = kernel_call(
        body,
        place,
        [*parts, reorder, *[saved] * (2 * planes), down, gate_up, first, second],
        specs,
        [*outs, bf16(rows, width_ff), bf16(rows, rank)],
        [
            *[
                pl.BlockSpec(
                    (*a.shape[:-1], columns),
                    lambda i, place, lead=(0,) * (len(a.shape) - 1): (*lead, outer(i)),
                )
                for a in outs
            ],
            pl.BlockSpec((rows, span), lambda i, place: (0, inner(i))),
            whole_of((rows, rank)),
        ],
        after,
        scratch=[
            pltpu.VMEM((rows, width), jnp.bfloat16),
            pltpu.VMEM((rows, rank), jnp.bfloat16),
            pltpu.VMEM((rows, 2 * width_ff), jnp.bfloat16),
            pltpu.VMEM((sides, columns, 2 * width_ff), jnp.bfloat16),
            pltpu.SemaphoreType.DMA((sides,)),
        ],
        steps=blocks + sides,
        name="expert",
        cost=8.0 + 4.5 * planes,
    )
    return result[:results], result[results], result[results + 1]


def adapter_gradients(place, groups, first, cells, pairs, after):
    rank, width_ff = first.shape
    width = groups[0][0][0].shape[-1]
    chunk = cells * pairs
    operands, sizes = [], []
    for parts, hidden, low in groups:
        operands += [*parts, hidden, low]
        sizes.append((len(parts), hidden.shape[0] // chunk))

    def body(place_ref, *refs):
        first_ref, grad_first_ref, grad_second_ref = refs[-3:]
        at = 0
        grad_first, grad_second = None, None
        for count, planes in sizes:
            parts, (hidden, low) = refs[at : at + count], refs[at + count : at + count + 2]
            at += count + 2
            low_in = contraction(hidden[...], first_ref[...], 1, 1).astype(jnp.bfloat16)
            if count == 1 and len(parts[0].shape) == 2:
                rows = parts[0][...]
            else:
                rows = jnp.concatenate(
                    [
                        chip_part(place_ref, parts, j)[i * cells : (i + 1) * cells, :]
                        for i in range(planes)
                        for j in range(pairs)
                    ],
                    axis=0,
                )
            part = contraction(low[...], hidden[...], 0, 0)
            grad_first = part if grad_first is None else grad_first + part
            part = contraction(low_in, rows, 0, 0)
            grad_second = part if grad_second is None else grad_second + part
        grad_first_ref[...] = adapter_scale * grad_first
        grad_second_ref[...] = adapter_scale * grad_second

    operands.append(first)
    outs = [f32(rank, width_ff), f32(rank, width)]
    return kernel_call(
        body,
        place,
        operands,
        [whole_of(a.shape) for a in operands],
        outs,
        [whole_of(a.shape) for a in outs],
        after,
        name="adapter_gradients",
        cost=6.0,
    )


def residual_messages(place, gradient, sums, folded, pairs, after):
    rows, width = gradient.shape
    rank = folded.shape[0]
    share, extra = width // pairs, rank // pairs
    count = len(sums)

    def body(place_ref, *refs):
        total = refs[0][...].astype(jnp.float32)
        for ref in refs[1 : count + 1]:
            total = total + ref[...].astype(jnp.float32)
        residual = total.astype(jnp.bfloat16)
        folded_ref, residual_ref = refs[count + 1], refs[count + 2]
        messages, term_ref = refs[count + 3 : count + 3 + pairs], refs[-1]
        residual_ref[...] = residual
        term = jnp.dot(folded_ref[...], residual, preferred_element_type=jnp.float32)
        term = (adapter_scale * term).astype(jnp.bfloat16)
        for number in range(pairs):
            term_ref[number] = term[:, number * share : (number + 1) * share]
        for j in range(pairs):
            messages[j][:rows, :] = residual
            part = term_ref[(place_ref[0] // 2) ^ j]
            for q in range(pairs):
                messages[j][rows:, q * share : (q + 1) * share] = part[q * extra : (q + 1) * extra]

    operands = [gradient, *sums, folded]
    outs = [bf16(rows, width)] + [bf16(rows + extra, width)] * pairs
    result = kernel_call(
        body,
        place,
        operands,
        [whole_of(a.shape) for a in operands],
        outs,
        [whole_of(a.shape) for a in outs],
        after,
        scratch=[pltpu.VMEM((pairs, rank, share), jnp.bfloat16)],
        name="residual_messages",
        cost=4.0,
    )
    return result[0], list(result[1:])


def head_gradients(place, numbers, own, other, weight, first, second, attended, pairs, after):
    width = own[0].shape[1]
    heads_width = weight.shape[0]
    rank = first.shape[0]
    share, extra = width // pairs, rank // pairs
    rows = own[0].shape[0] - extra
    count = len(numbers)

    def body(place_ref, *refs):
        weight_ref, first_ref, second_ref = refs[2 * count : 2 * count + 3]
        att_refs = refs[2 * count + 3 : 3 * count + 3]
        grad_refs = refs[3 * count + 3 : 4 * count + 3]
        term_ref, columns_ref = refs[4 * count + 3 :]
        core = place_ref[0] % 2
        total, columns = None, None
        for n in range(count):
            blocks = refs[n], refs[count + n]
            gradient = jnp.concatenate([ref[:rows, :] for ref in blocks], axis=0)
            low = contraction(gradient, second_ref[...], 1, 1).astype(jnp.bfloat16)
            result = contraction(gradient, weight_ref[...], 1, 1)
            result = result + adapter_scale * jnp.dot(
                low, first_ref[...], preferred_element_type=jnp.float32
            )
            grad_refs[n][...] = result.astype(jnp.bfloat16)
            for half in range(2):
                at = pl.ds(pl.multiple_of((core ^ half) * rows, rows), rows)
                part = contraction(low[half * rows : (half + 1) * rows], att_refs[n][at, :], 0, 0)
                total = part if total is None else total + part
            part = sum(ref[rows:, :].astype(jnp.float32) for ref in blocks)
            columns = part if columns is None else columns + part
        term_ref[...] = adapter_scale * total
        for q in range(pairs):
            columns_ref[q * extra : (q + 1) * extra, :] = columns[:, q * share : (q + 1) * share]

    operands = [*own, *other, weight, first, second, *[attended] * count]
    specs = [whole_of(a.shape) for a in operands[: 2 * count + 3]] + [
        pl.BlockSpec((2 * rows, heads_width), lambda i, place, j=j: ((place[0] // 2) ^ j, 0))
        for j in numbers
    ]
    outs = [*[bf16(2 * rows, heads_width)] * count, f32(rank, heads_width), f32(rank, share)]
    result = kernel_call(
        body,
        place,
        operands,
        specs,
        outs,
        [whole_of(a.shape) for a in outs],
        after,
        name="head_gradients",
        cost=2.5 + 2.2 * count,
    )
    return list(result[:count]), result[count], result[count + 1]


def forward_kernel(place, q_ref, k_ref, v_ref, a_ref, *refs):
    probs_ref, att_ref, folded = refs[-3:]
    head = pl.program_id(0)
    rows = q_ref.shape[0]
    token_block = folded.shape[2]
    block = min(256, rows)

    @pl.when(head == 0)
    def _():
        folded[...] = jnp.zeros_like(folded)

    for first in range(0, rows, block):
        last = first + block
        scores = contraction(q_ref[first:last, :], k_ref[:last, :], 1, 1) * att_scale
        row = first + lax.broadcasted_iota(jnp.int32, scores.shape, 0)
        column = lax.broadcasted_iota(jnp.int32, scores.shape, 1)
        scores = jnp.where(row >= column, scores, neg_big)
        weights = jnp.exp(scores - jnp.max(scores, axis=1, keepdims=True))
        weights = weights * (1.0 / jnp.sum(weights, axis=1, keepdims=True))
        low = weights.astype(jnp.bfloat16)
        probs_ref[0, first:last, :last] = low
        attended = jnp.dot(low, v_ref[:last, :], preferred_element_type=jnp.float32).astype(
            jnp.bfloat16
        )
        att_ref[first:last, :] = attended
        part = contraction(a_ref[...], attended, 1, 1).astype(jnp.bfloat16).astype(jnp.float32)
        for inner in range(0, block, token_block):
            number = (first + inner) // token_block
            folded[number] = folded[number] + part[:, inner : inner + token_block]


def attention_forward(place, queries, keys, values, first_factor, token_block, span, earlier, after):
    rows, width = queries.shape
    heads = width // HEAD_SIZE
    rank = first_factor.shape[0]
    start, count = span
    of_head = pl.BlockSpec((rows, HEAD_SIZE), lambda h, place: (0, start + h))
    of_group = pl.BlockSpec((rows, HEAD_SIZE), lambda h, place: (0, place[1]))
    part = (rows // token_block, rank, token_block)
    return pl.pallas_call(
        forward_kernel,
        grid_spec=pltpu.PrefetchScalarGridSpec(
            num_scalar_prefetch=1,
            grid=(count,),
            in_specs=[
                of_head,
                of_group,
                of_group,
                pl.BlockSpec((rank, HEAD_SIZE), lambda h, place: (0, start + h)),
                *unread(len(earlier) + len(after)),
            ],
            out_specs=[
                pl.BlockSpec((1, rows, rows), lambda h, place: (start + h, 0, 0)),
                of_head,
                pl.BlockSpec(part, lambda h, place: (0, 0, 0)),
            ],
        ),
        out_shape=[
            bf16(heads, rows, rows),
            bf16(rows, width),
            f32(*part),
        ],
        input_output_aliases={5 + n: n for n in range(len(earlier))},
        compiler_params=pltpu.CompilerParams(
            dimension_semantics=("arbitrary",), vmem_limit_bytes=VMEM_BYTES
        ),
        cost_estimate=estimate(2.2 * rows / 512 * count),
        name="attention_forward",
    )(place, queries, keys, values, first_factor, *earlier, *after)


def backward_kernel(place, q_ref, k_ref, v_ref, att_ref, probs_ref, *refs):
    dq_ref, even_ref, odd_ref, dk, dv, g_ref = refs[-6:]
    head = pl.program_id(0)
    rows = q_ref.shape[0]
    block = min(256, rows)
    pairs, token_block = even_ref.shape[:2]
    for j in range(pairs):
        for half in range(2):
            number = place[0] ^ (2 * j + half)
            at = pl.ds(pl.multiple_of(number * token_block, token_block), token_block)
            g_ref[at, :] = refs[j][half * token_block : (half + 1) * token_block, :]

    @pl.when(head == 0)
    def _():
        dk[...] = jnp.zeros_like(dk)
        dv[...] = jnp.zeros_like(dv)

    for first in range(0, rows, block):
        last = first + block
        gradient = g_ref[first:last, :]
        query = q_ref[first:last, :]
        probs = probs_ref[0, first:last, :last]
        grad_probs = contraction(gradient, v_ref[:last, :], 1, 1)
        delta = jnp.sum(
            gradient.astype(jnp.float32) * att_ref[first:last, :].astype(jnp.float32),
            axis=1,
            keepdims=True,
        )
        grad_scores = (probs.astype(jnp.float32) * (grad_probs - delta)).astype(jnp.bfloat16)
        dq_ref[first:last, :] = att_scale * jnp.dot(
            grad_scores, k_ref[:last, :], preferred_element_type=jnp.float32
        )
        dk[:last, :] += contraction(grad_scores, query, 0, 0)
        dv[:last, :] += contraction(probs, gradient, 0, 0)

    @pl.when(head == pl.num_programs(0) - 1)
    def _():
        for j in range(even_ref.shape[0]):
            for half, ref in enumerate((even_ref, odd_ref)):
                number = place[0] ^ (2 * j + half)
                at = pl.ds(pl.multiple_of(number * token_block, token_block), token_block)
                ref[j, :, :HEAD_SIZE] = (dk[at, :] * att_scale).astype(ref.dtype)
                ref[j, :, HEAD_SIZE:] = dv[at, :].astype(ref.dtype)


def attention_backward(place, queries, keys, values, attended, probs, gradients, token_block, after):
    rows, width = queries.shape
    heads = width // HEAD_SIZE
    pairs = rows // token_block // 2
    of_head = pl.BlockSpec((rows, HEAD_SIZE), lambda h, place: (0, h))
    of_group = pl.BlockSpec((rows, HEAD_SIZE), lambda h, place: (0, place[1]))
    part = pl.BlockSpec((pairs, token_block, 2 * HEAD_SIZE), lambda h, place: (0, 0, 0))
    part_shape = (pairs, token_block, 2 * HEAD_SIZE)
    return pl.pallas_call(
        backward_kernel,
        grid_spec=pltpu.PrefetchScalarGridSpec(
            num_scalar_prefetch=1,
            grid=(heads,),
            in_specs=[
                of_head,
                of_group,
                of_group,
                of_head,
                pl.BlockSpec((1, rows, rows), lambda h, place: (h, 0, 0)),
                *[pl.BlockSpec((2 * token_block, HEAD_SIZE), lambda h, place: (0, h))] * pairs,
                *unread(len(after)),
            ],
            out_specs=[of_head, part, part],
            scratch_shapes=[
                pltpu.VMEM((rows, HEAD_SIZE), jnp.float32),
                pltpu.VMEM((rows, HEAD_SIZE), jnp.float32),
                pltpu.VMEM((rows, HEAD_SIZE), jnp.bfloat16),
            ],
        ),
        out_shape=[
            jax.ShapeDtypeStruct((rows, width), jnp.float32),
            jax.ShapeDtypeStruct(part_shape, jnp.float32),
            jax.ShapeDtypeStruct(part_shape, jnp.bfloat16),
        ],
        compiler_params=pltpu.CompilerParams(
            dimension_semantics=("arbitrary",), vmem_limit_bytes=VMEM_BYTES
        ),
        cost_estimate=estimate(11.8),
        name="attention_backward",
    )(place, queries, keys, values, attended, probs, *gradients, *after)


def planes_sum(parts, grp_index):
    count = len(parts)
    total = None
    for plane in range(count):
        term = parts[0].astype(jnp.float32)
        for step in range(1, count):
            here = (grp_index - step) % count == plane
            term = jnp.where(here, parts[step].astype(jnp.float32), term)
        total = term if total is None else total + term
    return total


def on_device(
    output_gradient,
    expert_choice_index,
    routing_weight,
    stored_gate_preact,
    gate_up_weight,
    down_weight,
    down_first_factor,
    down_second_factor,
    rotated_queries,
    rotated_keys,
    stored_values,
    output_weight,
    output_first_factor,
    output_second_factor,
):
    tok_rows, model_width = output_gradient.shape
    top_count = expert_choice_index.shape[1]
    grp_count = lax.axis_size("grp")
    dev_count = lax.axis_size("dev")
    pairs = dev_count // 2
    experts = grp_count * dev_count
    slot_count = stored_gate_preact.shape[1]
    capacity = slot_count // experts
    cells = 2 * capacity
    chunk = dev_count * capacity
    grp_index = lax.axis_index("grp")
    dev_index = lax.axis_index("dev")
    heads = rotated_queries.shape[1] // HEAD_SIZE
    group_size = QUERY_HEADS // KVH
    planes = (grp_index - jnp.arange(grp_count, dtype=jnp.int32)) % grp_count
    place = jnp.concatenate(
        [jnp.stack([dev_index, dev_index * heads // group_size]).astype(jnp.int32), planes]
    )

    ring = sorted(range(1, grp_count), key=lambda s: (min(s, grp_count - s), s))
    middle = (2 * len(ring) + 2) // 3
    groups = [g for g in ([0], ring[:middle], ring[middle:]) if g]

    choice = jnp.concatenate(
        [expert_choice_index.T.astype(jnp.float32), routing_weight.T], axis=0
    )
    tokens = {0: output_gradient}
    near_tokens = {0: across(output_gradient, 1)}
    choice = jnp.stack([choice, across(choice, 1)])

    token = jnp.arange(tok_rows, dtype=jnp.int32)
    earlier = (token[:, None] < token[None, :]).astype(jnp.bfloat16)
    plane_experts = (
        grp_index * dev_count + (dev_index ^ (2 * jnp.arange(pairs, dtype=jnp.int32)))
    ).astype(jnp.float32)

    def table_of(choice):
        ids, weights = choice[:, :top_count], choice[:, top_count:]
        named = ids[:, :, None, :] == plane_experts[None, None, :, None]
        chosen = jnp.any(named, axis=1)
        weight_of = jnp.sum(jnp.where(named, weights[:, :, None, :], 0.0), axis=1)
        rank_of = lax.dot_general(
            chosen.astype(jnp.bfloat16),
            earlier,
            (((2,), (0,)), ((), ())),
            preferred_element_type=jnp.float32,
        )
        first_cell = jnp.arange(2, dtype=jnp.float32)[:, None, None] * capacity
        ranks = jnp.where(chosen, rank_of + first_cell, -1.0)
        return jnp.stack(
            [
                jnp.concatenate([ranks[0], ranks[1]], axis=1),
                jnp.concatenate([weight_of[0], weight_of[1]], axis=1),
            ]
        )

    tables = {0: table_of(choice)}

    line = jnp.arange(chunk, dtype=jnp.int32)
    saved_line = (dev_index ^ (line // capacity)) * capacity + line % capacity
    reorder = (saved_line[:, None] == line[None, :]).astype(jnp.bfloat16)

    aligned = cells % 16 == 0
    last = []

    chips = [[2 * j + core for j in range(pairs)] for core in range(2)]

    def exchanged(parts):
        if len(parts) == 1:
            return [
                lax.all_to_all(parts[0], "dev", 0, 0, axis_index_groups=chips, tiled=True)
            ]
        return [parts[0]] + [across(parts[j], 2 * j) for j in range(1, pairs)]

    def dispatched(group, stacked, extra=()):
        messages = dispatch(
            place,
            [tokens[s] for s in group],
            [near_tokens[s] for s in group],
            [tables[s] for s in group],
            cells,
            stacked and aligned,
            extra,
            last,
        )
        last[:] = messages[:1]
        return exchanged(messages)

    def worked(group, parts, stacked):
        count = len(group)
        rows = count * cells
        if not aligned:
            parts = [part.reshape(count, cells, model_width) for part in parts]
            parts = [jnp.concatenate(parts, axis=1).reshape(count * chunk, model_width)]
            outs = [bf16(count * chunk, model_width)]
        elif stacked:
            outs = [bf16(pairs, rows, model_width)]
        else:
            outs = [bf16(rows, model_width)] * pairs
        result, hidden, low = expert(
            place,
            group,
            parts,
            stored_gate_preact[0],
            reorder,
            down_weight[0],
            gate_up_weight[0],
            down_first_factor[0],
            down_second_factor[0],
            cells,
            pairs,
            outs,
            last,
        )
        last[:] = [result[0]]
        if not aligned:
            whole = result[0].reshape(count, pairs, cells, model_width)
            result = [whole[:, j].reshape(rows, model_width) for j in range(pairs)]
        return result, (parts, hidden, low)

    def combined(group, messages):
        owns, others = combine(place, messages, [tables[s] for s in group], tok_rows, last)
        last[:] = [others[0]]
        return [
            own + across(other, 1).astype(jnp.float32) for own, other in zip(owns, others)
        ]

    def forward(span, before):
        result = attention_forward(
            place,
            rotated_queries,
            rotated_keys,
            stored_values,
            output_first_factor,
            tok_rows,
            span,
            before,
            last,
        )
        last[:] = [result[2]]
        return result

    def sent_out(group, after):
        held = lax.optimization_barrier(((output_gradient, choice), after))[0]
        for s in group:
            choices[s] = shift(held[1], s)
        for s in group:
            tokens[s] = shift(held[0], s)

    def brought(group, after):
        held, _ = lax.optimization_barrier(
            ([tokens[s] for s in group], [choices[s] for s in group], last, after)
        )[:2], None
        for s, value, chosen in zip(group, *held):
            tokens[s] = value
            near_tokens[s] = across(value, 1)
            tables[s] = table_of(chosen)

    riding = aligned and len(groups) > 2
    half = heads // 2
    choices, arrived, finished, back = {}, {}, {}, {}
    sent_out(groups[1], [])
    arrived[0] = dispatched(groups[0], True)
    probs, attended, folded_a = forward((0, half), [])
    brought(groups[1], [])
    if len(groups) > 2:
        sent_out(groups[2], [tokens[s] for s in groups[1]])
    arrived[1] = dispatched(groups[1], True)
    finished[0] = worked(groups[0], arrived[0], True)
    probs, attended, folded_b = forward((half, heads - half), [probs, attended])
    if len(groups) > 2:
        brought(groups[2], [])
        arrived[2] = dispatched(groups[2], True, [folded_a, folded_b] if riding else [])
    for n in range(1, len(groups)):
        finished[n] = worked(groups[n], arrived[n], n == 2)
        rows = finished[n][0]
        if n == 1:
            back[1] = exchanged(rows)
            held, _ = lax.optimization_barrier((finished[0][0], (last, arrived[max(arrived)])))
            back[0] = exchanged(held)
        else:
            rows, _ = lax.optimization_barrier((rows, (back[0], back[1])))
            back[2] = exchanged(rows)

    def sent_home(group, totals, via):
        totals = {s: total.astype(jnp.bfloat16) for s, total in zip(group, totals)}
        return [shift(total, -via.get(s, s)) for s, total in totals.items()]

    totals = combined(groups[1], back[1])
    relayed = grp_count == 4
    if relayed:
        waiting = totals.pop(groups[1].index(1))
    sums = sent_home([s for s in groups[1] if s != 1 or not relayed], totals, {})
    own_sum = combined(groups[0], back[0])[0]
    if len(groups) > 2:
        back[2], sums = lax.optimization_barrier((back[2], sums))
        sums += sent_home(groups[2], combined(groups[2], back[2]), {2: 1} if relayed else {})
    if relayed:
        passed = (waiting + sums.pop().astype(jnp.float32)).astype(jnp.bfloat16)
        sums.append(shift(passed, -1))
        last[:] = lax.optimization_barrier((last, passed))[0]
    sums.append(own_sum)
    grad_first, grad_second = adapter_gradients(
        place, [finished[k][1] for k in finished], down_first_factor[0], cells, pairs, last
    )
    last[:] = [grad_first]

    if riding:
        folded = jnp.sum(arrived[2][0][:, cells * len(groups[2]) :].astype(jnp.float32), axis=0)
        folded = folded.reshape(folded.shape[0], 2, -1, tok_rows).transpose(1, 2, 0, 3)
        folded = folded.reshape(2, -1, tok_rows)
        folded = folded[0] + across(folded[1].astype(jnp.bfloat16), 1).astype(jnp.float32)
    else:
        folded = (folded_a + folded_b).astype(jnp.bfloat16)
        folded = lax.all_to_all(folded, "dev", 0, 0, tiled=True)
        folded = jnp.sum(folded.astype(jnp.float32), axis=0)
    folded = folded.astype(jnp.bfloat16)

    residual, near = residual_messages(place, output_gradient, sums, folded, pairs, last)
    near = near[:1] + [across(near[j], 2 * j) for j in range(1, pairs)]
    grads, term, columns = head_gradients(
        place,
        [0],
        near[:1],
        [across(near[0], 1)],
        output_weight,
        output_first_factor,
        output_second_factor,
        attended,
        pairs,
        last,
    )
    last[:] = grads
    held, _ = lax.optimization_barrier((near[1:], last))
    more, row_term, mine = head_gradients(
        place,
        list(range(1, pairs)),
        held,
        [across(part, 1) for part in held],
        output_weight,
        output_first_factor,
        output_second_factor,
        attended,
        pairs,
        last,
    )
    last[:] = more[:1]
    grads += more
    row_term = row_term + term
    mine = (mine + columns).astype(jnp.bfloat16)
    rank, share = mine.shape
    chip = dev_index // 2

    row_term = row_term.astype(jnp.bfloat16)
    if row_term.shape == mine.shape:
        terms = jnp.concatenate([row_term, mine], axis=0)
        terms = planes_sum([terms] + [shift(terms, s) for s in range(1, grp_count)], grp_index)
        output_first_gradient, mine = terms[:rank], terms[rank:]
    else:
        output_first_gradient = planes_sum(
            [row_term] + [shift(row_term, s) for s in range(1, grp_count)], grp_index
        )
        mine = planes_sum([mine] + [shift(mine, s) for s in range(1, grp_count)], grp_index)
    mine = mine.astype(jnp.bfloat16)

    query_gradient, pair_even, pair_odd = attention_backward(
        place,
        rotated_queries,
        rotated_keys,
        stored_values,
        attended,
        probs,
        grads,
        tok_rows,
        last,
    )
    both = (pair_even + across(pair_odd, 1).astype(jnp.float32)).astype(jnp.bfloat16)
    lanes = both.shape[2]
    flat = mine.reshape(rank * share // lanes, lanes)
    ends = [jnp.concatenate([both[j], flat], axis=0) for j in range(pairs)]
    ends = [ends[0]] + [across(ends[j], 2 * j) for j in range(1, pairs)]
    grads = []
    for group in range(KVH):
        grad = jnp.zeros((tok_rows, lanes), jnp.float32)
        for j in range(pairs):
            here = (dev_index ^ (2 * j)) * heads // group_size == group
            grad = grad + jnp.where(here, ends[j][:tok_rows].astype(jnp.float32), 0.0)
        grads.append(grad)
    key_gradient = jnp.concatenate([grad[:, :HEAD_SIZE] for grad in grads], axis=1)
    value_gradient = jnp.concatenate([grad[:, HEAD_SIZE:] for grad in grads], axis=1)
    second_columns = []
    for number in range(pairs):
        part = jnp.zeros((rank, share), jnp.float32)
        for j in range(pairs):
            value = ends[j][tok_rows:].astype(jnp.float32).reshape(rank, share)
            part = part + jnp.where(chip ^ j == number, value, 0.0)
        second_columns.append(part)
    output_second_gradient = jnp.concatenate(second_columns, axis=1)
    return (
        grad_first[None],
        grad_second[None],
        residual,
        output_first_gradient,
        output_second_gradient,
        query_gradient,
        key_gradient,
        value_gradient,
    )


def solution(mesh):
    in_specs = (
        P(("grp", "dev"), None),
        P(("grp", "dev"), None),
        P(("grp", "dev"), None),
        P(("grp", "dev"), None, None),
        P(("grp", "dev"), None, None),
        P(("grp", "dev"), None, None),
        P(("grp", "dev"), None, None),
        P(("grp", "dev"), None, None),
        P("grp", "dev"),
        P("grp", None),
        P("grp", None),
        P("dev", None),
        P(None, "dev"),
        P(),
    )
    out_specs = (
        P(("grp", "dev"), None, None),
        P(("grp", "dev"), None, None),
        P(("grp", "dev"), None),
        P(None, "dev"),
        P(),
        P("grp", "dev"),
        P(("grp", "dev"), None),
        P(("grp", "dev"), None),
    )
    return jax.shard_map(
        on_device, mesh=mesh, in_specs=in_specs, out_specs=out_specs, check_vma=False
    )
```

```python
import functools

import jax
import jax.numpy as jnp
from jax import lax
from jax.experimental import pallas as pl
from jax.experimental.pallas import tpu as pltpu
from jax.sharding import PartitionSpec as P

QUERY_HEADS = 32
KVH = 4
HEAD_SIZE = 128

adapter_scale = 2.0
neg_big = -1e30
att_scale = HEAD_SIZE ** (-0.5)
VMEM_BYTES = 36 * 1024 * 1024
COST_UNIT = 1000000


def contraction(left, right, left_dim, right_dim):
    return lax.dot_general(
        left, right, (((left_dim,), (right_dim,)), ((), ())), preferred_element_type=jnp.float32
    )


def across(value, step):
    count = lax.axis_size("dev")
    return lax.ppermute(value, "dev", [(i, i ^ step) for i in range(count)])


def shift(value, step):
    count = lax.axis_size("grp")
    return lax.ppermute(value, "grp", [(i, (i + step) % count) for i in range(count)])


def unread(count):
    return [pl.BlockSpec(memory_space=pl.ANY)] * count


def estimate(cost):
    return pl.CostEstimate(flops=0, bytes_accessed=int(cost * COST_UNIT), transcendentals=0)


def whole_of(shape):
    return pl.BlockSpec(shape, lambda i, place: (0,) * len(shape))


def kernel_call(
    body, place, operands, specs, outs, out_specs, after, scratch=(), steps=1, name=None, cost=1.0, held=0, far=True
):
    deps = len(after)
    after = in_hbm(*after) if far else after
    operands, specs = list(operands), list(specs)
    for n in range(held):
        operands[n] = pltpu.with_memory_space_constraint(operands[n], pltpu.VMEM)
        specs[n] = pl.BlockSpec(memory_space=pltpu.VMEM)

    def kernel(place_ref, *refs):
        count = len(operands)
        body(place_ref, *refs[:count], *refs[count + deps :])

    return pl.pallas_call(
        kernel,
        grid_spec=pltpu.PrefetchScalarGridSpec(
            num_scalar_prefetch=1,
            grid=(steps,),
            in_specs=[*specs, *unread(deps)],
            out_specs=out_specs,
            scratch_shapes=list(scratch),
        ),
        out_shape=outs,
        compiler_params=pltpu.CompilerParams(
            dimension_semantics=("arbitrary",), vmem_limit_bytes=VMEM_BYTES
        ),
        cost_estimate=estimate(cost),
        name=name,
    )(place, *operands, *after)


def in_hbm(*arrays):
    return [pltpu.with_memory_space_constraint(a, pltpu.HBM) for a in arrays]


def bf16(*shape):
    return pltpu.HBM(shape, jnp.bfloat16)


def f32(*shape):
    return pltpu.HBM(shape, jnp.float32)


def anywhere(*outs):
    return [jax.ShapeDtypeStruct(a.shape, a.dtype) for a in outs]


def filled_cells(ranks, count):
    cell = lax.broadcasted_iota(jnp.int32, (count, ranks.shape[1]), 0).astype(jnp.float32)
    return ranks == cell


def chip_part(place_ref, refs, j):
    return refs[0].at[(place_ref[0] // 2) ^ j] if len(refs) == 1 else refs[j]


def dispatch(place, own, other, tables, cells, stacked, extra, fresh, after):
    planes = len(own)
    pairs = tables[0].shape[1]
    width = own[0].shape[1]

    def body(place_ref, *refs):
        for i in range(planes):
            other_ref, own_ref, table_ref = refs[i], refs[planes + i], refs[2 * planes + i]
            tokens = jnp.concatenate([own_ref[...], other_ref[...]], axis=0)
            filled = [filled_cells(table_ref[0, j : j + 1, :], cells) for j in range(pairs)]
            weights = [
                jnp.sum(
                    jnp.where(filled[j], table_ref[1, j : j + 1, :], 0.0), axis=1, keepdims=True
                )
                for j in range(pairs)
            ]
            spread = jnp.concatenate([part.astype(jnp.bfloat16) for part in filled], axis=0)
            rows = jnp.dot(spread, tokens, preferred_element_type=jnp.float32)
            rows = (rows * jnp.concatenate(weights, axis=0)).astype(jnp.bfloat16)
            for j in range(pairs):
                out = chip_part(place_ref, refs[3 * planes + len(extra) :], j)
                out[i * cells : (i + 1) * cells, :] = rows[j * cells : (j + 1) * cells]

        if extra:
            parts = refs[3 * planes : 3 * planes + len(extra)]
            core = place_ref[0] % 2
            rank, lanes = extra[0].shape[1:]
            for chip in range(pairs):
                for half in range(2):
                    value = sum(ref[2 * chip + (core ^ half)] for ref in parts).astype(jnp.bfloat16)
                    for q in range(rank // added):
                        at = half * (width // 2) + q * lanes
                        refs[-1][chip, planes * cells :, at : at + lanes] = value[
                            q * added : (q + 1) * added
                        ]

    operands = [*other, *(own if fresh else in_hbm(*own)), *tables, *extra]
    added = 2 * extra[0].shape[1] * extra[0].shape[2] // width if extra else 0
    outs = [bf16(planes * cells, width)] * pairs
    if stacked:
        outs = [bf16(pairs, planes * cells + added, width)]
    return kernel_call(
        body,
        place,
        operands,
        [whole_of(a.shape) for a in operands],
        outs,
        [whole_of(a.shape) for a in outs],
        after,
        name="dispatch",
        held=2 * planes if fresh else planes,
        cost=3.5,
    )


def combine(place, messages, tables, token_block, after):
    planes = len(tables)
    pairs, both = tables[0].shape[1:]
    cells, width = messages[0].shape[-2] // planes, messages[0].shape[-1]
    count = len(messages)

    def body(place_ref, *refs):
        for i in range(planes):
            table_ref = refs[count + i]
            own_ref, other_ref = refs[count + planes + 2 * i : count + planes + 2 * i + 2]
            spread = jnp.concatenate(
                [
                    filled_cells(table_ref[0, j : j + 1, :], cells).astype(jnp.bfloat16)
                    for j in range(pairs)
                ],
                axis=0,
            )
            rows = [
                chip_part(place_ref, refs[:count], j)[i * cells : (i + 1) * cells, :]
                for j in range(pairs)
            ]
            total = contraction(spread, jnp.concatenate(rows, axis=0), 0, 0)
            own_ref[...] = total[:token_block]
            other_ref[...] = total[token_block:].astype(jnp.bfloat16)

    operands = [*messages, *tables]
    outs = [f32(token_block, width), bf16(both - token_block, width)] * planes
    result = kernel_call(
        body,
        place,
        operands,
        [whole_of(a.shape) for a in operands],
        outs,
        [whole_of(a.shape) for a in outs],
        after,
        name="combine",
        held=count,
        cost=4.5,
    )
    return result[::2], result[1::2]


def expert(place, steps, parts, saved, reorder, down, gate_up, first, second, cells, pairs, outs, after):
    planes = len(steps)
    chunk = cells * pairs
    rows = planes * chunk
    width_ff, width = down.shape
    rank = first.shape[0]
    span = 256
    blocks = width_ff // span
    sides = 2
    columns = width // sides
    count, results = len(parts), len(outs)
    split_in = count > 1 or parts[0].ndim == 3
    split_out = results > 1 or len(outs[0].shape) == 3

    def body(place_ref, *refs):
        rows_in = refs[:count]
        reorder_ref = refs[count]
        gates = refs[count + 1 : count + 1 + planes]
        ups = refs[count + 1 + planes : count + 1 + 2 * planes]
        down_ref, back_ref, first_ref, second_ref = refs[count + 1 + 2 * planes :][:4]
        rest = refs[count + 5 + 2 * planes :]
        rows_out, (hidden_ref, low_ref) = rest[:results], rest[results : results + 2]
        routed, low_grad, grad_pre, back, arrived = rest[results + 2 :]
        number = pl.program_id(0)

        def fetch(side):
            at = pl.ds(side * columns, columns)
            return pltpu.make_async_copy(back_ref.at[at, :], back.at[side], arrived.at[side])

        @pl.when(number == 0)
        def _():
            for side in range(sides):
                fetch(side).start()
            if split_in:
                for i in range(planes):
                    for j in range(pairs):
                        at = i * chunk + j * cells
                        part = chip_part(place_ref, rows_in, j)
                        routed[at : at + cells, :] = part[i * cells : (i + 1) * cells, :]
            else:
                routed[...] = rows_in[0][...]
            low = contraction(routed[...], second_ref[...], 1, 1).astype(jnp.bfloat16)
            low_grad[...] = low
            low_ref[...] = low

        for block in range(blocks):

            @pl.when(number == block)
            def _():
                order = reorder_ref[...]
                gate = [
                    jnp.dot(order, ref[...], preferred_element_type=jnp.float32) for ref in gates
                ]
                up = [jnp.dot(order, ref[...], preferred_element_type=jnp.float32) for ref in ups]
                gate = jnp.concatenate(gate, axis=0) if planes > 1 else gate[0]
                up = jnp.concatenate(up, axis=0) if planes > 1 else up[0]
                sigmoid = jax.nn.sigmoid(gate)
                active = gate * sigmoid
                slope = sigmoid * (1.0 + gate * (1.0 - sigmoid))
                hidden_ref[...] = (active * up).astype(jnp.bfloat16)
                grad_hidden = contraction(
                    routed[...], down_ref[...], 1, 1
                ) + adapter_scale * jnp.dot(
                    low_grad[...], first_ref[...], preferred_element_type=jnp.float32
                )
                at = block * span
                grad_pre[:, at : at + span] = (grad_hidden * up * slope).astype(jnp.bfloat16)
                grad_pre[:, width_ff + at : width_ff + at + span] = (grad_hidden * active).astype(
                    jnp.bfloat16
                )

        for side in range(sides):

            @pl.when(number == blocks + side)
            def _():
                fetch(side).wait()
                result = contraction(grad_pre[...], back[side], 1, 1).astype(jnp.bfloat16)
                if split_out:
                    for i in range(planes):
                        for j in range(pairs):
                            at = i * chunk + j * cells
                            part = chip_part(place_ref, rows_out, j)
                            part[i * cells : (i + 1) * cells, :] = result[at : at + cells]
                else:
                    rows_out[0][...] = result

    def inner(i):
        return jnp.minimum(i, blocks - 1)

    def outer(i):
        return jnp.maximum(i - blocks, 0)

    def saved_block(step, offset):
        return pl.BlockSpec(
            (chunk, span), lambda i, place: (place[2 + step], offset + inner(i))
        )

    specs = [
        *[whole_of(a.shape) for a in parts],
        whole_of(reorder.shape),
        *[saved_block(step, 0) for step in steps],
        *[saved_block(step, blocks) for step in steps],
        pl.BlockSpec((span, width), lambda i, place: (inner(i), 0)),
        pl.BlockSpec(memory_space=pl.ANY),
        pl.BlockSpec((rank, span), lambda i, place: (0, inner(i))),
        whole_of(second.shape),
    ]
    result = kernel_call(
        body,
        place,
        [*parts, reorder, *in_hbm(*[saved] * (2 * planes), down, gate_up, first, second)],
        specs,
        [*outs, bf16(rows, width_ff), bf16(rows, rank)],
        [
            *[
                pl.BlockSpec(
                    (*a.shape[:-1], columns),
                    lambda i, place, lead=(0,) * (len(a.shape) - 1): (*lead, outer(i)),
                )
                for a in outs
            ],
            pl.BlockSpec((rows, span), lambda i, place: (0, inner(i))),
            whole_of((rows, rank)),
        ],
        after,
        scratch=[
            pltpu.VMEM((rows, width), jnp.bfloat16),
            pltpu.VMEM((rows, rank), jnp.bfloat16),
            pltpu.VMEM((rows, 2 * width_ff), jnp.bfloat16),
            pltpu.VMEM((sides, columns, 2 * width_ff), jnp.bfloat16),
            pltpu.SemaphoreType.DMA((sides,)),
        ],
        steps=blocks + sides,
        name="expert",
        held=count,
        cost=8.0 + 4.5 * planes,
    )
    return result[:results], result[results], result[results + 1]


def adapter_gradients(place, groups, first, cells, pairs, after):
    rank, width_ff = first.shape
    width = groups[0][0][0].shape[-1]
    chunk = cells * pairs
    operands, sizes = [], []
    for parts, hidden, low in groups:
        operands += [*parts, hidden, low]
        sizes.append((len(parts), hidden.shape[0] // chunk))

    def body(place_ref, *refs):
        first_ref, grad_first_ref, grad_second_ref = refs[-3:]
        at = 0
        grad_first, grad_second = None, None
        for count, planes in sizes:
            parts, (hidden, low) = refs[at : at + count], refs[at + count : at + count + 2]
            at += count + 2
            low_in = contraction(hidden[...], first_ref[...], 1, 1).astype(jnp.bfloat16)
            if count == 1 and len(parts[0].shape) == 2:
                rows = parts[0][...]
            else:
                rows = jnp.concatenate(
                    [
                        chip_part(place_ref, parts, j)[i * cells : (i + 1) * cells, :]
                        for i in range(planes)
                        for j in range(pairs)
                    ],
                    axis=0,
                )
            part = contraction(low[...], hidden[...], 0, 0)
            grad_first = part if grad_first is None else grad_first + part
            part = contraction(low_in, rows, 0, 0)
            grad_second = part if grad_second is None else grad_second + part
        grad_first_ref[...] = adapter_scale * grad_first
        grad_second_ref[...] = adapter_scale * grad_second

    operands += in_hbm(first)
    outs = [f32(rank, width_ff), f32(rank, width)]
    return kernel_call(
        body,
        place,
        operands,
        [whole_of(a.shape) for a in operands],
        outs,
        [whole_of(a.shape) for a in outs],
        after,
        name="adapter_gradients",
        cost=6.0,
    )


def residual_messages(place, gradient, sums, folded, pairs, after):
    rows, width = gradient.shape
    rank = folded.shape[0]
    share, extra = width // pairs, rank // pairs
    count = len(sums)

    def body(place_ref, *refs):
        total = refs[0][...].astype(jnp.float32)
        for ref in refs[1 : count + 1]:
            total = total + ref[...].astype(jnp.float32)
        residual = total.astype(jnp.bfloat16)
        folded_ref, residual_ref = refs[count + 1], refs[count + 2]
        messages, term_ref = refs[count + 3 : count + 3 + pairs], refs[-1]
        residual_ref[...] = residual
        term = jnp.dot(folded_ref[...], residual, preferred_element_type=jnp.float32)
        term = (adapter_scale * term).astype(jnp.bfloat16)
        for number in range(pairs):
            term_ref[number] = term[:, number * share : (number + 1) * share]
        for j in range(pairs):
            messages[j][:rows, :] = residual
            part = term_ref[(place_ref[0] // 2) ^ j]
            for q in range(pairs):
                messages[j][rows:, q * share : (q + 1) * share] = part[q * extra : (q + 1) * extra]

    operands = [gradient, *sums, folded]
    outs = anywhere(bf16(rows, width), *[bf16(rows + extra, width)] * pairs)
    result = kernel_call(
        body,
        place,
        operands,
        [whole_of(a.shape) for a in operands],
        outs,
        [whole_of(a.shape) for a in outs],
        after,
        scratch=[pltpu.VMEM((pairs, rank, share), jnp.bfloat16)],
        name="residual_messages",
        held=count + 1,
        cost=4.0,
    )
    return result[0], list(result[1:])


def head_gradients(place, numbers, own, other, weight, first, second, attended, pairs, after):
    width = own[0].shape[1]
    heads_width = weight.shape[0]
    rank = first.shape[0]
    share, extra = width // pairs, rank // pairs
    rows = own[0].shape[0] - extra
    count = len(numbers)

    def body(place_ref, *refs):
        weight_ref, first_ref, second_ref = refs[2 * count : 2 * count + 3]
        att_refs = refs[2 * count + 3 : 3 * count + 3]
        grad_refs = refs[3 * count + 3 : 4 * count + 3]
        term_ref, columns_ref = refs[4 * count + 3 :]
        core = place_ref[0] % 2
        total, columns = None, None
        for n in range(count):
            blocks = refs[n], refs[count + n]
            gradient = jnp.concatenate([ref[:rows, :] for ref in blocks], axis=0)
            low = contraction(gradient, second_ref[...], 1, 1).astype(jnp.bfloat16)
            result = contraction(gradient, weight_ref[...], 1, 1)
            result = result + adapter_scale * jnp.dot(
                low, first_ref[...], preferred_element_type=jnp.float32
            )
            grad_refs[n][...] = result.astype(jnp.bfloat16)
            for half in range(2):
                at = pl.ds(pl.multiple_of((core ^ half) * rows, rows), rows)
                part = contraction(low[half * rows : (half + 1) * rows], att_refs[n][at, :], 0, 0)
                total = part if total is None else total + part
            part = sum(ref[rows:, :].astype(jnp.float32) for ref in blocks)
            columns = part if columns is None else columns + part
        term_ref[...] = adapter_scale * total
        for q in range(pairs):
            columns_ref[q * extra : (q + 1) * extra, :] = columns[:, q * share : (q + 1) * share]

    operands = [*own, *other, *in_hbm(weight, first, second, *[attended] * count)]
    specs = [whole_of(a.shape) for a in operands[: 2 * count + 3]] + [
        pl.BlockSpec((2 * rows, heads_width), lambda i, place, j=j: ((place[0] // 2) ^ j, 0))
        for j in numbers
    ]
    outs = anywhere(
        *[bf16(2 * rows, heads_width)] * count, f32(rank, heads_width), f32(rank, share)
    )
    result = kernel_call(
        body,
        place,
        operands,
        specs,
        outs,
        [whole_of(a.shape) for a in outs],
        after,
        name="head_gradients",
        held=2 * count,
        far=False,
        cost=2.5 + 2.2 * count,
    )
    return list(result[:count]), result[count], result[count + 1]


def forward_kernel(place, q_ref, k_ref, v_ref, a_ref, *refs):
    probs_ref, att_ref, folded = refs[-3:]
    head = pl.program_id(0)
    rows = q_ref.shape[0]
    token_block = folded.shape[2]
    block = min(256, rows)

    @pl.when(head == 0)
    def _():
        folded[...] = jnp.zeros_like(folded)

    for first in range(0, rows, block):
        last = first + block
        scores = contraction(q_ref[first:last, :], k_ref[:last, :], 1, 1) * att_scale
        row = first + lax.broadcasted_iota(jnp.int32, scores.shape, 0)
        column = lax.broadcasted_iota(jnp.int32, scores.shape, 1)
        scores = jnp.where(row >= column, scores, neg_big)
        weights = jnp.exp(scores - jnp.max(scores, axis=1, keepdims=True))
        weights = weights * (1.0 / jnp.sum(weights, axis=1, keepdims=True))
        low = weights.astype(jnp.bfloat16)
        probs_ref[0, first:last, :last] = low
        attended = jnp.dot(low, v_ref[:last, :], preferred_element_type=jnp.float32).astype(
            jnp.bfloat16
        )
        att_ref[first:last, :] = attended
        part = contraction(a_ref[...], attended, 1, 1).astype(jnp.bfloat16).astype(jnp.float32)
        for inner in range(0, block, token_block):
            number = (first + inner) // token_block
            folded[number] = folded[number] + part[:, inner : inner + token_block]


def attention_forward(place, queries, keys, values, first_factor, token_block, span, earlier, after):
    rows, width = queries.shape
    heads = width // HEAD_SIZE
    rank = first_factor.shape[0]
    start, count = span
    of_head = pl.BlockSpec((rows, HEAD_SIZE), lambda h, place: (0, start + h))
    of_group = pl.BlockSpec((rows, HEAD_SIZE), lambda h, place: (0, place[1]))
    part = (rows // token_block, rank, token_block)
    return pl.pallas_call(
        forward_kernel,
        grid_spec=pltpu.PrefetchScalarGridSpec(
            num_scalar_prefetch=1,
            grid=(count,),
            in_specs=[
                of_head,
                of_group,
                of_group,
                pl.BlockSpec((rank, HEAD_SIZE), lambda h, place: (0, start + h)),
                *unread(len(earlier) + len(after)),
            ],
            out_specs=[
                pl.BlockSpec((1, rows, rows), lambda h, place: (start + h, 0, 0)),
                of_head,
                pl.BlockSpec(part, lambda h, place: (0, 0, 0)),
            ],
        ),
        out_shape=[
            bf16(heads, rows, rows),
            bf16(rows, width),
            f32(*part),
        ],
        input_output_aliases={5 + n: n for n in range(len(earlier))},
        compiler_params=pltpu.CompilerParams(
            dimension_semantics=("arbitrary",), vmem_limit_bytes=VMEM_BYTES
        ),
        cost_estimate=estimate(2.2 * rows / 512 * count),
        name="attention_forward",
    )(place, *in_hbm(queries, keys, values, first_factor), *earlier, *after)


def backward_kernel(place, q_ref, k_ref, v_ref, att_ref, probs_ref, *refs):
    dq_ref, even_ref, odd_ref, dk, dv, g_ref = refs[-6:]
    head = pl.program_id(0)
    rows = q_ref.shape[0]
    block = min(256, rows)
    pairs, token_block = even_ref.shape[:2]
    for j in range(pairs):
        for half in range(2):
            number = place[0] ^ (2 * j + half)
            at = pl.ds(pl.multiple_of(number * token_block, token_block), token_block)
            g_ref[at, :] = refs[j][half * token_block : (half + 1) * token_block, :]

    @pl.when(head == 0)
    def _():
        dk[...] = jnp.zeros_like(dk)
        dv[...] = jnp.zeros_like(dv)

    for first in range(0, rows, block):
        last = first + block
        gradient = g_ref[first:last, :]
        query = q_ref[first:last, :]
        probs = probs_ref[0, first:last, :last]
        grad_probs = contraction(gradient, v_ref[:last, :], 1, 1)
        delta = jnp.sum(
            gradient.astype(jnp.float32) * att_ref[first:last, :].astype(jnp.float32),
            axis=1,
            keepdims=True,
        )
        grad_scores = (probs.astype(jnp.float32) * (grad_probs - delta)).astype(jnp.bfloat16)
        dq_ref[first:last, :] = att_scale * jnp.dot(
            grad_scores, k_ref[:last, :], preferred_element_type=jnp.float32
        )
        dk[:last, :] += contraction(grad_scores, query, 0, 0)
        dv[:last, :] += contraction(probs, gradient, 0, 0)

    @pl.when(head == pl.num_programs(0) - 1)
    def _():
        for j in range(even_ref.shape[0]):
            for half, ref in enumerate((even_ref, odd_ref)):
                number = place[0] ^ (2 * j + half)
                at = pl.ds(pl.multiple_of(number * token_block, token_block), token_block)
                ref[j, :, :HEAD_SIZE] = (dk[at, :] * att_scale).astype(ref.dtype)
                ref[j, :, HEAD_SIZE:] = dv[at, :].astype(ref.dtype)


def attention_backward(place, queries, keys, values, attended, probs, gradients, token_block, after):
    rows, width = queries.shape
    heads = width // HEAD_SIZE
    pairs = rows // token_block // 2
    of_head = pl.BlockSpec((rows, HEAD_SIZE), lambda h, place: (0, h))
    of_group = pl.BlockSpec((rows, HEAD_SIZE), lambda h, place: (0, place[1]))
    part = pl.BlockSpec((pairs, token_block, 2 * HEAD_SIZE), lambda h, place: (0, 0, 0))
    part_shape = (pairs, token_block, 2 * HEAD_SIZE)
    return pl.pallas_call(
        backward_kernel,
        grid_spec=pltpu.PrefetchScalarGridSpec(
            num_scalar_prefetch=1,
            grid=(heads,),
            in_specs=[
                of_head,
                of_group,
                of_group,
                of_head,
                pl.BlockSpec((1, rows, rows), lambda h, place: (h, 0, 0)),
                *[pl.BlockSpec((2 * token_block, HEAD_SIZE), lambda h, place: (0, h))] * pairs,
                *unread(len(after)),
            ],
            out_specs=[of_head, part, part],
            scratch_shapes=[
                pltpu.VMEM((rows, HEAD_SIZE), jnp.float32),
                pltpu.VMEM((rows, HEAD_SIZE), jnp.float32),
                pltpu.VMEM((rows, HEAD_SIZE), jnp.bfloat16),
            ],
        ),
        out_shape=[
            jax.ShapeDtypeStruct((rows, width), jnp.float32),
            jax.ShapeDtypeStruct(part_shape, jnp.float32),
            jax.ShapeDtypeStruct(part_shape, jnp.bfloat16),
        ],
        compiler_params=pltpu.CompilerParams(
            dimension_semantics=("arbitrary",), vmem_limit_bytes=VMEM_BYTES
        ),
        cost_estimate=estimate(11.8),
        name="attention_backward",
    )(place, *in_hbm(queries, keys, values, attended, probs), *gradients, *after)


def planes_sum(parts, grp_index):
    count = len(parts)
    total = None
    for plane in range(count):
        term = parts[0].astype(jnp.float32)
        for step in range(1, count):
            here = (grp_index - step) % count == plane
            term = jnp.where(here, parts[step].astype(jnp.float32), term)
        total = term if total is None else total + term
    return total


def on_device(
    output_gradient,
    expert_choice_index,
    routing_weight,
    stored_gate_preact,
    gate_up_weight,
    down_weight,
    down_first_factor,
    down_second_factor,
    rotated_queries,
    rotated_keys,
    stored_values,
    output_weight,
    output_first_factor,
    output_second_factor,
):
    tok_rows, model_width = output_gradient.shape
    top_count = expert_choice_index.shape[1]
    grp_count = lax.axis_size("grp")
    dev_count = lax.axis_size("dev")
    pairs = dev_count // 2
    experts = grp_count * dev_count
    slot_count = stored_gate_preact.shape[1]
    capacity = slot_count // experts
    cells = 2 * capacity
    chunk = dev_count * capacity
    grp_index = lax.axis_index("grp")
    dev_index = lax.axis_index("dev")
    heads = rotated_queries.shape[1] // HEAD_SIZE
    group_size = QUERY_HEADS // KVH
    planes = (grp_index - jnp.arange(grp_count, dtype=jnp.int32)) % grp_count
    place = jnp.concatenate(
        [jnp.stack([dev_index, dev_index * heads // group_size]).astype(jnp.int32), planes]
    )

    ring = sorted(range(1, grp_count), key=lambda s: (min(s, grp_count - s), s))
    middle = (2 * len(ring) + 2) // 3
    groups = [g for g in ([0], ring[:middle], ring[middle:]) if g]

    choice = jnp.concatenate(
        [expert_choice_index.T.astype(jnp.float32), routing_weight.T], axis=0
    )
    tokens = {0: output_gradient}
    near_tokens = {0: across(output_gradient, 1)}
    choice = jnp.stack([choice, across(choice, 1)])

    token = jnp.arange(tok_rows, dtype=jnp.int32)
    earlier = (token[:, None] < token[None, :]).astype(jnp.bfloat16)
    plane_experts = (
        grp_index * dev_count + (dev_index ^ (2 * jnp.arange(pairs, dtype=jnp.int32)))
    ).astype(jnp.float32)

    def table_of(choice):
        ids, weights = choice[:, :top_count], choice[:, top_count:]
        named = ids[:, :, None, :] == plane_experts[None, None, :, None]
        chosen = jnp.any(named, axis=1)
        weight_of = jnp.sum(jnp.where(named, weights[:, :, None, :], 0.0), axis=1)
        rank_of = lax.dot_general(
            chosen.astype(jnp.bfloat16),
            earlier,
            (((2,), (0,)), ((), ())),
            preferred_element_type=jnp.float32,
        )
        first_cell = jnp.arange(2, dtype=jnp.float32)[:, None, None] * capacity
        ranks = jnp.where(chosen, rank_of + first_cell, -1.0)
        return jnp.stack(
            [
                jnp.concatenate([ranks[0], ranks[1]], axis=1),
                jnp.concatenate([weight_of[0], weight_of[1]], axis=1),
            ]
        )

    tables = {0: table_of(choice)}

    line = jnp.arange(chunk, dtype=jnp.int32)
    saved_line = (dev_index ^ (line // capacity)) * capacity + line % capacity
    reorder = (saved_line[:, None] == line[None, :]).astype(jnp.bfloat16)

    aligned = cells % 16 == 0
    last = []

    chips = [[2 * j + core for j in range(pairs)] for core in range(2)]

    def exchanged(parts):
        if len(parts) == 1:
            return [
                lax.all_to_all(parts[0], "dev", 0, 0, axis_index_groups=chips, tiled=True)
            ]
        return [parts[0]] + [across(parts[j], 2 * j) for j in range(1, pairs)]

    def dispatched(group, stacked, extra=()):
        messages = dispatch(
            place,
            [tokens[s] for s in group],
            [near_tokens[s] for s in group],
            [tables[s] for s in group],
            cells,
            stacked and aligned,
            extra,
            group != [0],
            last,
        )
        last[:] = messages[:1]
        return exchanged(messages)

    def worked(group, parts, stacked):
        count = len(group)
        rows = count * cells
        if not aligned:
            parts = [part.reshape(count, cells, model_width) for part in parts]
            parts = [jnp.concatenate(parts, axis=1).reshape(count * chunk, model_width)]
            outs = [bf16(count * chunk, model_width)]
        elif stacked:
            outs = [bf16(pairs, rows, model_width)]
        else:
            outs = [bf16(rows, model_width)] * pairs
        result, hidden, low = expert(
            place,
            group,
            parts,
            stored_gate_preact[0],
            reorder,
            down_weight[0],
            gate_up_weight[0],
            down_first_factor[0],
            down_second_factor[0],
            cells,
            pairs,
            outs,
            last,
        )
        last[:] = [result[0]]
        if not aligned:
            whole = result[0].reshape(count, pairs, cells, model_width)
            result = [whole[:, j].reshape(rows, model_width) for j in range(pairs)]
        return result, (parts, hidden, low)

    def combined(group, messages):
        owns, others = combine(place, messages, [tables[s] for s in group], tok_rows, last)
        last[:] = [others[0]]
        return [
            own + across(other, 1).astype(jnp.float32) for own, other in zip(owns, others)
        ]

    def forward(span, before):
        result = attention_forward(
            place,
            rotated_queries,
            rotated_keys,
            stored_values,
            output_first_factor,
            tok_rows,
            span,
            before,
            last,
        )
        last[:] = [result[2]]
        return result

    def sent_out(group, after):
        held = lax.optimization_barrier(((output_gradient, choice), after))[0]
        for s in group:
            choices[s] = shift(held[1], s)
        for s in group:
            tokens[s] = shift(held[0], s)

    def brought(group, after):
        held, _ = lax.optimization_barrier(
            ([tokens[s] for s in group], [choices[s] for s in group], last, after)
        )[:2], None
        for s, value, chosen in zip(group, *held):
            tokens[s] = value
            near_tokens[s] = across(value, 1)
            tables[s] = table_of(chosen)

    riding = aligned and len(groups) > 2
    half = heads // 2
    choices, arrived, finished, back = {}, {}, {}, {}
    sent_out(groups[1], [])
    arrived[0] = dispatched(groups[0], True)
    probs, attended, folded_a = forward((0, half), [])
    brought(groups[1], [])
    if len(groups) > 2:
        sent_out(groups[2], [tokens[s] for s in groups[1]])
    arrived[1] = dispatched(groups[1], True)
    finished[0] = worked(groups[0], arrived[0], True)
    probs, attended, folded_b = forward((half, heads - half), [probs, attended])
    if len(groups) > 2:
        brought(groups[2], [])
        arrived[2] = dispatched(groups[2], True, [folded_a, folded_b] if riding else [])
    for n in range(1, len(groups)):
        finished[n] = worked(groups[n], arrived[n], n == 2)
        rows = finished[n][0]
        if n == 1:
            back[1] = exchanged(rows)
        else:
            back[2] = exchanged(rows)
    held, _ = lax.optimization_barrier((finished[0][0], back[max(back)]))
    back[0] = exchanged(held)

    def sent_home(group, totals, via):
        totals = {s: total.astype(jnp.bfloat16) for s, total in zip(group, totals)}
        return [shift(total, -via.get(s, s)) for s, total in totals.items()]

    totals = combined(groups[1], back[1])
    relayed = grp_count == 4
    if relayed:
        waiting = totals.pop(groups[1].index(1))
    sums = sent_home([s for s in groups[1] if s != 1 or not relayed], totals, {})
    if len(groups) > 2:
        back[0], sums = lax.optimization_barrier((back[0], sums))
        sums += sent_home(groups[2], combined(groups[2], back[2]), {2: 1} if relayed else {})
    if relayed:
        passed = (waiting + sums.pop().astype(jnp.float32)).astype(jnp.bfloat16)
        sums.append(shift(passed, -1))
        last[:] = lax.optimization_barrier((last, passed))[0]
    sums.append(combined(groups[0], back[0])[0])
    grad_first, grad_second = adapter_gradients(
        place, [finished[k][1] for k in finished], down_first_factor[0], cells, pairs, last
    )
    last[:] = [grad_first]

    if riding:
        folded = jnp.sum(arrived[2][0][:, cells * len(groups[2]) :].astype(jnp.float32), axis=0)
        folded = folded.reshape(folded.shape[0], 2, -1, tok_rows).transpose(1, 2, 0, 3)
        folded = folded.reshape(2, -1, tok_rows)
        folded = folded[0] + across(folded[1].astype(jnp.bfloat16), 1).astype(jnp.float32)
    else:
        folded = (folded_a + folded_b).astype(jnp.bfloat16)
        folded = lax.all_to_all(folded, "dev", 0, 0, tiled=True)
        folded = jnp.sum(folded.astype(jnp.float32), axis=0)
    folded = folded.astype(jnp.bfloat16)

    residual, near = residual_messages(place, output_gradient, sums, folded, pairs, last)
    near = near[:1] + [across(near[j], 2 * j) for j in range(1, pairs)]
    grads, term, columns = head_gradients(
        place,
        [0],
        near[:1],
        [across(near[0], 1)],
        output_weight,
        output_first_factor,
        output_second_factor,
        attended,
        pairs,
        last,
    )
    last[:] = grads
    held, _ = lax.optimization_barrier((near[1:], last))
    more, row_term, mine = head_gradients(
        place,
        list(range(1, pairs)),
        held,
        [across(part, 1) for part in held],
        output_weight,
        output_first_factor,
        output_second_factor,
        attended,
        pairs,
        last,
    )
    last[:] = more[:1]
    grads += more
    row_term = row_term + term
    mine = (mine + columns).astype(jnp.bfloat16)
    rank, share = mine.shape
    chip = dev_index // 2

    row_term = row_term.astype(jnp.bfloat16)
    if row_term.shape == mine.shape:
        terms = jnp.concatenate([row_term, mine], axis=0)
        terms = planes_sum([terms] + [shift(terms, s) for s in range(1, grp_count)], grp_index)
        output_first_gradient, mine = terms[:rank], terms[rank:]
    else:
        output_first_gradient = planes_sum(
            [row_term] + [shift(row_term, s) for s in range(1, grp_count)], grp_index
        )
        mine = planes_sum([mine] + [shift(mine, s) for s in range(1, grp_count)], grp_index)
    mine = mine.astype(jnp.bfloat16)

    query_gradient, pair_even, pair_odd = attention_backward(
        place,
        rotated_queries,
        rotated_keys,
        stored_values,
        attended,
        probs,
        grads,
        tok_rows,
        last,
    )
    both = (pair_even + across(pair_odd, 1).astype(jnp.float32)).astype(jnp.bfloat16)
    lanes = both.shape[2]
    flat = mine.reshape(rank * share // lanes, lanes)
    ends = [jnp.concatenate([both[j], flat], axis=0) for j in range(pairs)]
    ends = [ends[0]] + [across(ends[j], 2 * j) for j in range(1, pairs)]
    grads = []
    for group in range(KVH):
        grad = jnp.zeros((tok_rows, lanes), jnp.float32)
        for j in range(pairs):
            here = (dev_index ^ (2 * j)) * heads // group_size == group
            grad = grad + jnp.where(here, ends[j][:tok_rows].astype(jnp.float32), 0.0)
        grads.append(grad)
    key_gradient = jnp.concatenate([grad[:, :HEAD_SIZE] for grad in grads], axis=1)
    value_gradient = jnp.concatenate([grad[:, HEAD_SIZE:] for grad in grads], axis=1)
    second_columns = []
    for number in range(pairs):
        part = jnp.zeros((rank, share), jnp.float32)
        for j in range(pairs):
            value = ends[j][tok_rows:].astype(jnp.float32).reshape(rank, share)
            part = part + jnp.where(chip ^ j == number, value, 0.0)
        second_columns.append(part)
    output_second_gradient = jnp.concatenate(second_columns, axis=1)
    return (
        grad_first[None],
        grad_second[None],
        residual,
        output_first_gradient,
        output_second_gradient,
        query_gradient,
        key_gradient,
        value_gradient,
    )


def solution(mesh):
    in_specs = (
        P(("grp", "dev"), None),
        P(("grp", "dev"), None),
        P(("grp", "dev"), None),
        P(("grp", "dev"), None, None),
        P(("grp", "dev"), None, None),
        P(("grp", "dev"), None, None),
        P(("grp", "dev"), None, None),
        P(("grp", "dev"), None, None),
        P("grp", "dev"),
        P("grp", None),
        P("grp", None),
        P("dev", None),
        P(None, "dev"),
        P(),
    )
    out_specs = (
        P(("grp", "dev"), None, None),
        P(("grp", "dev"), None, None),
        P(("grp", "dev"), None),
        P(None, "dev"),
        P(),
        P("grp", "dev"),
        P(("grp", "dev"), None),
        P(("grp", "dev"), None),
    )
    return jax.shard_map(
        on_device, mesh=mesh, in_specs=in_specs, out_specs=out_specs, check_vma=False
    )
```

```python
import functools

import jax
import jax.numpy as jnp
from jax import lax
from jax.experimental import pallas as pl
from jax.experimental.pallas import tpu as pltpu
from jax.sharding import PartitionSpec as P

QUERY_HEADS = 32
KVH = 4
HEAD_SIZE = 128

adapter_scale = 2.0
neg_big = -1e30
att_scale = HEAD_SIZE ** (-0.5)
VMEM_BYTES = 36 * 1024 * 1024
COST_UNIT = 1000000


def contraction(left, right, left_dim, right_dim):
    return lax.dot_general(
        left, right, (((left_dim,), (right_dim,)), ((), ())), preferred_element_type=jnp.float32
    )


def across(value, step):
    count = lax.axis_size("dev")
    return lax.ppermute(value, "dev", [(i, i ^ step) for i in range(count)])


def shift(value, step):
    count = lax.axis_size("grp")
    return lax.ppermute(value, "grp", [(i, (i + step) % count) for i in range(count)])


def unread(count):
    return [pl.BlockSpec(memory_space=pl.ANY)] * count


def estimate(cost):
    return pl.CostEstimate(flops=0, bytes_accessed=int(cost * COST_UNIT), transcendentals=0)


def whole_of(shape):
    return pl.BlockSpec(shape, lambda i, place: (0,) * len(shape))


def kernel_call(
    body, place, operands, specs, outs, out_specs, after, scratch=(), steps=1, name=None, cost=1.0, held=0, far=True
):
    deps = len(after)
    after = in_hbm(*after) if far else after
    operands, specs = list(operands), list(specs)
    for n in range(held):
        operands[n] = pltpu.with_memory_space_constraint(operands[n], pltpu.VMEM)
        specs[n] = pl.BlockSpec(memory_space=pltpu.VMEM)

    def kernel(place_ref, *refs):
        count = len(operands)
        body(place_ref, *refs[:count], *refs[count + deps :])

    return pl.pallas_call(
        kernel,
        grid_spec=pltpu.PrefetchScalarGridSpec(
            num_scalar_prefetch=1,
            grid=(steps,),
            in_specs=[*specs, *unread(deps)],
            out_specs=out_specs,
            scratch_shapes=list(scratch),
        ),
        out_shape=outs,
        compiler_params=pltpu.CompilerParams(
            dimension_semantics=("arbitrary",), vmem_limit_bytes=VMEM_BYTES
        ),
        cost_estimate=estimate(cost),
        name=name,
    )(place, *operands, *after)


def in_hbm(*arrays):
    return [pltpu.with_memory_space_constraint(a, pltpu.HBM) for a in arrays]


def bf16(*shape):
    return pltpu.HBM(shape, jnp.bfloat16)


def f32(*shape):
    return pltpu.HBM(shape, jnp.float32)


def anywhere(*outs):
    return [jax.ShapeDtypeStruct(a.shape, a.dtype) for a in outs]


def filled_cells(ranks, count):
    cell = lax.broadcasted_iota(jnp.int32, (count, ranks.shape[1]), 0).astype(jnp.float32)
    return ranks == cell


def chip_part(place_ref, refs, j):
    return refs[0].at[(place_ref[0] // 2) ^ j] if len(refs) == 1 else refs[j]


def dispatch(place, own, other, tables, cells, stacked, extra, fresh, after):
    planes = len(own)
    pairs = tables[0].shape[1]
    width = own[0].shape[1]

    def body(place_ref, *refs):
        for i in range(planes):
            other_ref, own_ref, table_ref = refs[i], refs[planes + i], refs[2 * planes + i]
            tokens = jnp.concatenate([own_ref[...], other_ref[...]], axis=0)
            filled = [filled_cells(table_ref[0, j : j + 1, :], cells) for j in range(pairs)]
            weights = [
                jnp.sum(
                    jnp.where(filled[j], table_ref[1, j : j + 1, :], 0.0), axis=1, keepdims=True
                )
                for j in range(pairs)
            ]
            spread = jnp.concatenate([part.astype(jnp.bfloat16) for part in filled], axis=0)
            rows = jnp.dot(spread, tokens, preferred_element_type=jnp.float32)
            rows = (rows * jnp.concatenate(weights, axis=0)).astype(jnp.bfloat16)
            for j in range(pairs):
                out = chip_part(place_ref, refs[3 * planes + len(extra) :], j)
                out[i * cells : (i + 1) * cells, :] = rows[j * cells : (j + 1) * cells]

        if extra:
            parts = refs[3 * planes : 3 * planes + len(extra)]
            core = place_ref[0] % 2
            rank, lanes = extra[0].shape[1:]
            for chip in range(pairs):
                for half in range(2):
                    value = sum(ref[2 * chip + (core ^ half)] for ref in parts).astype(jnp.bfloat16)
                    for q in range(rank // added):
                        at = half * (width // 2) + q * lanes
                        refs[-1][chip, planes * cells :, at : at + lanes] = value[
                            q * added : (q + 1) * added
                        ]

    operands = [*other, *(own if fresh else in_hbm(*own)), *tables, *extra]
    added = 2 * extra[0].shape[1] * extra[0].shape[2] // width if extra else 0
    outs = [bf16(planes * cells, width)] * pairs
    if stacked:
        outs = [bf16(pairs, planes * cells + added, width)]
    return kernel_call(
        body,
        place,
        operands,
        [whole_of(a.shape) for a in operands],
        outs,
        [whole_of(a.shape) for a in outs],
        after,
        name="dispatch",
        held=2 * planes if fresh else planes,
        cost=3.5,
    )


def combine(place, messages, tables, token_block, after):
    planes = len(tables)
    pairs, both = tables[0].shape[1:]
    cells, width = messages[0].shape[-2] // planes, messages[0].shape[-1]
    count = len(messages)

    def body(place_ref, *refs):
        for i in range(planes):
            table_ref = refs[count + i]
            own_ref, other_ref = refs[count + planes + 2 * i : count + planes + 2 * i + 2]
            spread = jnp.concatenate(
                [
                    filled_cells(table_ref[0, j : j + 1, :], cells).astype(jnp.bfloat16)
                    for j in range(pairs)
                ],
                axis=0,
            )
            rows = [
                chip_part(place_ref, refs[:count], j)[i * cells : (i + 1) * cells, :]
                for j in range(pairs)
            ]
            total = contraction(spread, jnp.concatenate(rows, axis=0), 0, 0)
            own_ref[...] = total[:token_block]
            other_ref[...] = total[token_block:].astype(jnp.bfloat16)

    operands = [*messages, *tables]
    outs = [f32(token_block, width), bf16(both - token_block, width)] * planes
    result = kernel_call(
        body,
        place,
        operands,
        [whole_of(a.shape) for a in operands],
        outs,
        [whole_of(a.shape) for a in outs],
        after,
        name="combine",
        held=count,
        cost=4.5,
    )
    return result[::2], result[1::2]


def expert(place, steps, parts, saved, reorder, down, gate_up, first, second, cells, pairs, outs, after):
    planes = len(steps)
    chunk = cells * pairs
    rows = planes * chunk
    width_ff, width = down.shape
    rank = first.shape[0]
    span = 256
    blocks = width_ff // span
    sides = 2
    columns = width // sides
    count, results = len(parts), len(outs)
    split_in = count > 1 or parts[0].ndim == 3
    split_out = results > 1 or len(outs[0].shape) == 3

    def body(place_ref, *refs):
        rows_in = refs[:count]
        reorder_ref = refs[count]
        gates = refs[count + 1 : count + 1 + planes]
        ups = refs[count + 1 + planes : count + 1 + 2 * planes]
        down_ref, back_ref, first_ref, second_ref = refs[count + 1 + 2 * planes :][:4]
        rest = refs[count + 5 + 2 * planes :]
        rows_out, (hidden_ref, low_ref) = rest[:results], rest[results : results + 2]
        routed, low_grad, grad_pre, back, arrived = rest[results + 2 :]
        number = pl.program_id(0)

        def fetch(side):
            at = pl.ds(side * columns, columns)
            return pltpu.make_async_copy(back_ref.at[at, :], back.at[side], arrived.at[side])

        @pl.when(number == 0)
        def _():
            for side in range(sides):
                fetch(side).start()
            if split_in:
                for i in range(planes):
                    for j in range(pairs):
                        at = i * chunk + j * cells
                        part = chip_part(place_ref, rows_in, j)
                        routed[at : at + cells, :] = part[i * cells : (i + 1) * cells, :]
            else:
                routed[...] = rows_in[0][...]
            low = contraction(routed[...], second_ref[...], 1, 1).astype(jnp.bfloat16)
            low_grad[...] = low
            low_ref[...] = low

        for block in range(blocks):

            @pl.when(number == block)
            def _():
                order = reorder_ref[...]
                gate = [
                    jnp.dot(order, ref[...], preferred_element_type=jnp.float32) for ref in gates
                ]
                up = [jnp.dot(order, ref[...], preferred_element_type=jnp.float32) for ref in ups]
                gate = jnp.concatenate(gate, axis=0) if planes > 1 else gate[0]
                up = jnp.concatenate(up, axis=0) if planes > 1 else up[0]
                sigmoid = jax.nn.sigmoid(gate)
                active = gate * sigmoid
                slope = sigmoid * (1.0 + gate * (1.0 - sigmoid))
                hidden_ref[...] = (active * up).astype(jnp.bfloat16)
                grad_hidden = contraction(
                    routed[...], down_ref[...], 1, 1
                ) + adapter_scale * jnp.dot(
                    low_grad[...], first_ref[...], preferred_element_type=jnp.float32
                )
                at = block * span
                grad_pre[:, at : at + span] = (grad_hidden * up * slope).astype(jnp.bfloat16)
                grad_pre[:, width_ff + at : width_ff + at + span] = (grad_hidden * active).astype(
                    jnp.bfloat16
                )

        for side in range(sides):

            @pl.when(number == blocks + side)
            def _():
                fetch(side).wait()
                result = contraction(grad_pre[...], back[side], 1, 1).astype(jnp.bfloat16)
                if split_out:
                    for i in range(planes):
                        for j in range(pairs):
                            at = i * chunk + j * cells
                            part = chip_part(place_ref, rows_out, j)
                            part[i * cells : (i + 1) * cells, :] = result[at : at + cells]
                else:
                    rows_out[0][...] = result

    def inner(i):
        return jnp.minimum(i, blocks - 1)

    def outer(i):
        return jnp.maximum(i - blocks, 0)

    def saved_block(step, offset):
        return pl.BlockSpec(
            (chunk, span), lambda i, place: (place[2 + step], offset + inner(i))
        )

    specs = [
        *[whole_of(a.shape) for a in parts],
        whole_of(reorder.shape),
        *[saved_block(step, 0) for step in steps],
        *[saved_block(step, blocks) for step in steps],
        pl.BlockSpec((span, width), lambda i, place: (inner(i), 0)),
        pl.BlockSpec(memory_space=pl.ANY),
        pl.BlockSpec((rank, span), lambda i, place: (0, inner(i))),
        whole_of(second.shape),
    ]
    result = kernel_call(
        body,
        place,
        [*parts, reorder, *in_hbm(*[saved] * (2 * planes), down, gate_up, first, second)],
        specs,
        [*outs, bf16(rows, width_ff), bf16(rows, rank)],
        [
            *[
                pl.BlockSpec(
                    (*a.shape[:-1], columns),
                    lambda i, place, lead=(0,) * (len(a.shape) - 1): (*lead, outer(i)),
                )
                for a in outs
            ],
            pl.BlockSpec((rows, span), lambda i, place: (0, inner(i))),
            whole_of((rows, rank)),
        ],
        after,
        scratch=[
            pltpu.VMEM((rows, width), jnp.bfloat16),
            pltpu.VMEM((rows, rank), jnp.bfloat16),
            pltpu.VMEM((rows, 2 * width_ff), jnp.bfloat16),
            pltpu.VMEM((sides, columns, 2 * width_ff), jnp.bfloat16),
            pltpu.SemaphoreType.DMA((sides,)),
        ],
        steps=blocks + sides,
        name="expert",
        held=count,
        cost=8.0 + 4.5 * planes,
    )
    return result[:results], result[results], result[results + 1]


def adapter_gradients(place, groups, first, cells, pairs, after):
    rank, width_ff = first.shape
    width = groups[0][0][0].shape[-1]
    chunk = cells * pairs
    operands, sizes = [], []
    for parts, hidden, low in groups:
        operands += [*parts, hidden, low]
        sizes.append((len(parts), hidden.shape[0] // chunk))

    def body(place_ref, *refs):
        first_ref, grad_first_ref, grad_second_ref = refs[-3:]
        at = 0
        grad_first, grad_second = None, None
        for count, planes in sizes:
            parts, (hidden, low) = refs[at : at + count], refs[at + count : at + count + 2]
            at += count + 2
            low_in = contraction(hidden[...], first_ref[...], 1, 1).astype(jnp.bfloat16)
            if count == 1 and len(parts[0].shape) == 2:
                rows = parts[0][...]
            else:
                rows = jnp.concatenate(
                    [
                        chip_part(place_ref, parts, j)[i * cells : (i + 1) * cells, :]
                        for i in range(planes)
                        for j in range(pairs)
                    ],
                    axis=0,
                )
            part = contraction(low[...], hidden[...], 0, 0)
            grad_first = part if grad_first is None else grad_first + part
            part = contraction(low_in, rows, 0, 0)
            grad_second = part if grad_second is None else grad_second + part
        grad_first_ref[...] = adapter_scale * grad_first
        grad_second_ref[...] = adapter_scale * grad_second

    operands += in_hbm(first)
    outs = [f32(rank, width_ff), f32(rank, width)]
    return kernel_call(
        body,
        place,
        operands,
        [whole_of(a.shape) for a in operands],
        outs,
        [whole_of(a.shape) for a in outs],
        after,
        name="adapter_gradients",
        cost=6.0,
    )


def residual_messages(place, gradient, sums, folded, pairs, after):
    rows, width = gradient.shape
    rank = folded.shape[0]
    share, extra = width // pairs, rank // pairs
    count = len(sums)

    def body(place_ref, *refs):
        total = refs[0][...].astype(jnp.float32)
        for ref in refs[1 : count + 1]:
            total = total + ref[...].astype(jnp.float32)
        residual = total.astype(jnp.bfloat16)
        folded_ref, residual_ref = refs[count + 1], refs[count + 2]
        messages, term_ref = refs[count + 3 : count + 3 + pairs], refs[-1]
        residual_ref[...] = residual
        term = jnp.dot(folded_ref[...], residual, preferred_element_type=jnp.float32)
        term = (adapter_scale * term).astype(jnp.bfloat16)
        for number in range(pairs):
            term_ref[number] = term[:, number * share : (number + 1) * share]
        for j in range(pairs):
            messages[j][:rows, :] = residual
            part = term_ref[(place_ref[0] // 2) ^ j]
            for q in range(pairs):
                messages[j][rows:, q * share : (q + 1) * share] = part[q * extra : (q + 1) * extra]

    operands = [gradient, *sums, folded]
    outs = anywhere(bf16(rows, width), *[bf16(rows + extra, width)] * pairs)
    result = kernel_call(
        body,
        place,
        operands,
        [whole_of(a.shape) for a in operands],
        outs,
        [whole_of(a.shape) for a in outs],
        after,
        scratch=[pltpu.VMEM((pairs, rank, share), jnp.bfloat16)],
        name="residual_messages",
        held=count + 1,
        cost=4.0,
    )
    return result[0], list(result[1:])


def head_gradients(place, numbers, own, other, weight, first, second, attended, pairs, after):
    width = own[0].shape[1]
    heads_width = weight.shape[0]
    rank = first.shape[0]
    share, extra = width // pairs, rank // pairs
    rows = own[0].shape[0] - extra
    count = len(numbers)

    def body(place_ref, *refs):
        weight_ref, first_ref, second_ref = refs[2 * count : 2 * count + 3]
        att_refs = refs[2 * count + 3 : 3 * count + 3]
        grad_refs = refs[3 * count + 3 : 4 * count + 3]
        term_ref, columns_ref = refs[4 * count + 3 :]
        core = place_ref[0] % 2
        total, columns = None, None
        for n in range(count):
            blocks = refs[n], refs[count + n]
            gradient = jnp.concatenate([ref[:rows, :] for ref in blocks], axis=0)
            low = contraction(gradient, second_ref[...], 1, 1).astype(jnp.bfloat16)
            result = contraction(gradient, weight_ref[...], 1, 1)
            result = result + adapter_scale * jnp.dot(
                low, first_ref[...], preferred_element_type=jnp.float32
            )
            grad_refs[n][...] = result.astype(jnp.bfloat16)
            for half in range(2):
                at = pl.ds(pl.multiple_of((core ^ half) * rows, rows), rows)
                part = contraction(low[half * rows : (half + 1) * rows], att_refs[n][at, :], 0, 0)
                total = part if total is None else total + part
            part = sum(ref[rows:, :].astype(jnp.float32) for ref in blocks)
            columns = part if columns is None else columns + part
        term_ref[...] = adapter_scale * total
        for q in range(pairs):
            columns_ref[q * extra : (q + 1) * extra, :] = columns[:, q * share : (q + 1) * share]

    operands = [*own, *other, *in_hbm(weight, first, second, *[attended] * count)]
    specs = [whole_of(a.shape) for a in operands[: 2 * count + 3]] + [
        pl.BlockSpec((2 * rows, heads_width), lambda i, place, j=j: ((place[0] // 2) ^ j, 0))
        for j in numbers
    ]
    outs = anywhere(
        *[bf16(2 * rows, heads_width)] * count, f32(rank, heads_width), f32(rank, share)
    )
    result = kernel_call(
        body,
        place,
        operands,
        specs,
        outs,
        [whole_of(a.shape) for a in outs],
        after,
        name="head_gradients",
        held=2 * count,
        far=False,
        cost=2.5 + 2.2 * count,
    )
    return list(result[:count]), result[count], result[count + 1]


def forward_kernel(place, q_ref, k_ref, v_ref, a_ref, *refs):
    probs_ref, att_ref, folded = refs[-3:]
    head = pl.program_id(0)
    rows = q_ref.shape[0]
    token_block = folded.shape[2]
    block = min(256, rows)

    @pl.when(head == 0)
    def _():
        folded[...] = jnp.zeros_like(folded)

    for first in range(0, rows, block):
        last = first + block
        scores = contraction(q_ref[first:last, :], k_ref[:last, :], 1, 1) * att_scale
        row = first + lax.broadcasted_iota(jnp.int32, scores.shape, 0)
        column = lax.broadcasted_iota(jnp.int32, scores.shape, 1)
        scores = jnp.where(row >= column, scores, neg_big)
        weights = jnp.exp(scores - jnp.max(scores, axis=1, keepdims=True))
        weights = weights * (1.0 / jnp.sum(weights, axis=1, keepdims=True))
        low = weights.astype(jnp.bfloat16)
        probs_ref[0, first:last, :last] = low
        attended = jnp.dot(low, v_ref[:last, :], preferred_element_type=jnp.float32).astype(
            jnp.bfloat16
        )
        att_ref[first:last, :] = attended
        part = contraction(a_ref[...], attended, 1, 1).astype(jnp.bfloat16).astype(jnp.float32)
        for inner in range(0, block, token_block):
            number = (first + inner) // token_block
            folded[number] = folded[number] + part[:, inner : inner + token_block]


def attention_forward(place, queries, keys, values, first_factor, token_block, span, earlier, after):
    rows, width = queries.shape
    heads = width // HEAD_SIZE
    rank = first_factor.shape[0]
    start, count = span
    of_head = pl.BlockSpec((rows, HEAD_SIZE), lambda h, place: (0, start + h))
    of_group = pl.BlockSpec((rows, HEAD_SIZE), lambda h, place: (0, place[1]))
    part = (rows // token_block, rank, token_block)
    return pl.pallas_call(
        forward_kernel,
        grid_spec=pltpu.PrefetchScalarGridSpec(
            num_scalar_prefetch=1,
            grid=(count,),
            in_specs=[
                of_head,
                of_group,
                of_group,
                pl.BlockSpec((rank, HEAD_SIZE), lambda h, place: (0, start + h)),
                *unread(len(earlier) + len(after)),
            ],
            out_specs=[
                pl.BlockSpec((1, rows, rows), lambda h, place: (start + h, 0, 0)),
                of_head,
                pl.BlockSpec(part, lambda h, place: (0, 0, 0)),
            ],
        ),
        out_shape=[
            bf16(heads, rows, rows),
            bf16(rows, width),
            f32(*part),
        ],
        input_output_aliases={5 + n: n for n in range(len(earlier))},
        compiler_params=pltpu.CompilerParams(
            dimension_semantics=("arbitrary",), vmem_limit_bytes=VMEM_BYTES
        ),
        cost_estimate=estimate(2.2 * rows / 512 * count),
        name="attention_forward",
    )(place, *in_hbm(queries, keys, values, first_factor), *earlier, *after)


def backward_kernel(place, q_ref, k_ref, v_ref, att_ref, probs_ref, *refs):
    dq_ref, even_ref, odd_ref, dk, dv, g_ref = refs[-6:]
    head = pl.program_id(0)
    rows = q_ref.shape[0]
    block = min(256, rows)
    pairs, token_block = even_ref.shape[:2]
    for j in range(pairs):
        for half in range(2):
            number = place[0] ^ (2 * j + half)
            at = pl.ds(pl.multiple_of(number * token_block, token_block), token_block)
            g_ref[at, :] = refs[j][half * token_block : (half + 1) * token_block, :]

    @pl.when(head == 0)
    def _():
        dk[...] = jnp.zeros_like(dk)
        dv[...] = jnp.zeros_like(dv)

    for first in range(0, rows, block):
        last = first + block
        gradient = g_ref[first:last, :]
        query = q_ref[first:last, :]
        probs = probs_ref[0, first:last, :last]
        grad_probs = contraction(gradient, v_ref[:last, :], 1, 1)
        delta = jnp.sum(
            gradient.astype(jnp.float32) * att_ref[first:last, :].astype(jnp.float32),
            axis=1,
            keepdims=True,
        )
        grad_scores = (probs.astype(jnp.float32) * (grad_probs - delta)).astype(jnp.bfloat16)
        dq_ref[first:last, :] = att_scale * jnp.dot(
            grad_scores, k_ref[:last, :], preferred_element_type=jnp.float32
        )
        dk[:last, :] += contraction(grad_scores, query, 0, 0)
        dv[:last, :] += contraction(probs, gradient, 0, 0)

    @pl.when(head == pl.num_programs(0) - 1)
    def _():
        for j in range(even_ref.shape[0]):
            for half, ref in enumerate((even_ref, odd_ref)):
                number = place[0] ^ (2 * j + half)
                at = pl.ds(pl.multiple_of(number * token_block, token_block), token_block)
                ref[j, :, :HEAD_SIZE] = (dk[at, :] * att_scale).astype(ref.dtype)
                ref[j, :, HEAD_SIZE:] = dv[at, :].astype(ref.dtype)


def attention_backward(place, queries, keys, values, attended, probs, gradients, token_block, after):
    rows, width = queries.shape
    heads = width // HEAD_SIZE
    pairs = rows // token_block // 2
    of_head = pl.BlockSpec((rows, HEAD_SIZE), lambda h, place: (0, h))
    of_group = pl.BlockSpec((rows, HEAD_SIZE), lambda h, place: (0, place[1]))
    part = pl.BlockSpec((pairs, token_block, 2 * HEAD_SIZE), lambda h, place: (0, 0, 0))
    part_shape = (pairs, token_block, 2 * HEAD_SIZE)
    return pl.pallas_call(
        backward_kernel,
        grid_spec=pltpu.PrefetchScalarGridSpec(
            num_scalar_prefetch=1,
            grid=(heads,),
            in_specs=[
                of_head,
                of_group,
                of_group,
                of_head,
                pl.BlockSpec((1, rows, rows), lambda h, place: (h, 0, 0)),
                *[pl.BlockSpec((2 * token_block, HEAD_SIZE), lambda h, place: (0, h))] * pairs,
                *unread(len(after)),
            ],
            out_specs=[of_head, part, part],
            scratch_shapes=[
                pltpu.VMEM((rows, HEAD_SIZE), jnp.float32),
                pltpu.VMEM((rows, HEAD_SIZE), jnp.float32),
                pltpu.VMEM((rows, HEAD_SIZE), jnp.bfloat16),
            ],
        ),
        out_shape=[
            jax.ShapeDtypeStruct((rows, width), jnp.float32),
            jax.ShapeDtypeStruct(part_shape, jnp.float32),
            jax.ShapeDtypeStruct(part_shape, jnp.bfloat16),
        ],
        compiler_params=pltpu.CompilerParams(
            dimension_semantics=("arbitrary",), vmem_limit_bytes=VMEM_BYTES
        ),
        cost_estimate=estimate(11.8),
        name="attention_backward",
    )(place, *in_hbm(queries, keys, values, attended, probs), *gradients, *after)


def planes_sum(parts, grp_index):
    count = len(parts)
    total = None
    for plane in range(count):
        term = parts[0].astype(jnp.float32)
        for step in range(1, count):
            here = (grp_index - step) % count == plane
            term = jnp.where(here, parts[step].astype(jnp.float32), term)
        total = term if total is None else total + term
    return total


def on_device(
    output_gradient,
    expert_choice_index,
    routing_weight,
    stored_gate_preact,
    gate_up_weight,
    down_weight,
    down_first_factor,
    down_second_factor,
    rotated_queries,
    rotated_keys,
    stored_values,
    output_weight,
    output_first_factor,
    output_second_factor,
):
    tok_rows, model_width = output_gradient.shape
    top_count = expert_choice_index.shape[1]
    grp_count = lax.axis_size("grp")
    dev_count = lax.axis_size("dev")
    pairs = dev_count // 2
    experts = grp_count * dev_count
    slot_count = stored_gate_preact.shape[1]
    capacity = slot_count // experts
    cells = 2 * capacity
    chunk = dev_count * capacity
    grp_index = lax.axis_index("grp")
    dev_index = lax.axis_index("dev")
    heads = rotated_queries.shape[1] // HEAD_SIZE
    group_size = QUERY_HEADS // KVH
    planes = (grp_index - jnp.arange(grp_count, dtype=jnp.int32)) % grp_count
    place = jnp.concatenate(
        [jnp.stack([dev_index, dev_index * heads // group_size]).astype(jnp.int32), planes]
    )

    ring = sorted(range(1, grp_count), key=lambda s: (min(s, grp_count - s), s))
    middle = (2 * len(ring) + 2) // 3
    groups = [g for g in ([0], ring[:middle], ring[middle:]) if g]

    choice = jnp.concatenate(
        [expert_choice_index.T.astype(jnp.float32), routing_weight.T], axis=0
    )
    tokens = {0: output_gradient}
    near_tokens = {0: across(output_gradient, 1)}
    choice = jnp.stack([choice, across(choice, 1)])

    token = jnp.arange(tok_rows, dtype=jnp.int32)
    earlier = (token[:, None] < token[None, :]).astype(jnp.bfloat16)
    plane_experts = (
        grp_index * dev_count + (dev_index ^ (2 * jnp.arange(pairs, dtype=jnp.int32)))
    ).astype(jnp.float32)

    def table_of(choice):
        ids, weights = choice[:, :top_count], choice[:, top_count:]
        named = ids[:, :, None, :] == plane_experts[None, None, :, None]
        chosen = jnp.any(named, axis=1)
        weight_of = jnp.sum(jnp.where(named, weights[:, :, None, :], 0.0), axis=1)
        rank_of = lax.dot_general(
            chosen.astype(jnp.bfloat16),
            earlier,
            (((2,), (0,)), ((), ())),
            preferred_element_type=jnp.float32,
        )
        first_cell = jnp.arange(2, dtype=jnp.float32)[:, None, None] * capacity
        ranks = jnp.where(chosen, rank_of + first_cell, -1.0)
        return jnp.stack(
            [
                jnp.concatenate([ranks[0], ranks[1]], axis=1),
                jnp.concatenate([weight_of[0], weight_of[1]], axis=1),
            ]
        )

    tables = {0: table_of(choice)}

    line = jnp.arange(chunk, dtype=jnp.int32)
    saved_line = (dev_index ^ (line // capacity)) * capacity + line % capacity
    reorder = (saved_line[:, None] == line[None, :]).astype(jnp.bfloat16)

    aligned = cells % 16 == 0
    last = []

    chips = [[2 * j + core for j in range(pairs)] for core in range(2)]

    def exchanged(parts):
        if len(parts) == 1:
            return [
                lax.all_to_all(parts[0], "dev", 0, 0, axis_index_groups=chips, tiled=True)
            ]
        return [parts[0]] + [across(parts[j], 2 * j) for j in range(1, pairs)]

    def dispatched(group, stacked, extra=()):
        messages = dispatch(
            place,
            [tokens[s] for s in group],
            [near_tokens[s] for s in group],
            [tables[s] for s in group],
            cells,
            stacked and aligned,
            extra,
            group != [0],
            last,
        )
        last[:] = messages[:1]
        return exchanged(messages)

    def worked(group, parts, stacked):
        count = len(group)
        rows = count * cells
        if not aligned:
            parts = [part.reshape(count, cells, model_width) for part in parts]
            parts = [jnp.concatenate(parts, axis=1).reshape(count * chunk, model_width)]
            outs = [bf16(count * chunk, model_width)]
        elif stacked:
            outs = [bf16(pairs, rows, model_width)]
        else:
            outs = [bf16(rows, model_width)] * pairs
        result, hidden, low = expert(
            place,
            group,
            parts,
            stored_gate_preact[0],
            reorder,
            down_weight[0],
            gate_up_weight[0],
            down_first_factor[0],
            down_second_factor[0],
            cells,
            pairs,
            outs,
            last,
        )
        last[:] = [result[0]]
        if not aligned:
            whole = result[0].reshape(count, pairs, cells, model_width)
            result = [whole[:, j].reshape(rows, model_width) for j in range(pairs)]
        return result, (parts, hidden, low)

    def combined(group, messages):
        owns, others = combine(place, messages, [tables[s] for s in group], tok_rows, last)
        last[:] = [others[0]]
        return [
            own + across(other, 1).astype(jnp.float32) for own, other in zip(owns, others)
        ]

    def forward(span, before):
        result = attention_forward(
            place,
            rotated_queries,
            rotated_keys,
            stored_values,
            output_first_factor,
            tok_rows,
            span,
            before,
            last,
        )
        last[:] = [result[2]]
        return result

    def sent_out(group, after):
        held = lax.optimization_barrier(((output_gradient, choice), after))[0]
        for s in group:
            choices[s] = shift(held[1], s)
        for s in group:
            tokens[s] = shift(held[0], s)

    def brought(group, after):
        held, _ = lax.optimization_barrier(
            ([tokens[s] for s in group], [choices[s] for s in group], last, after)
        )[:2], None
        for s, value, chosen in zip(group, *held):
            tokens[s] = value
            near_tokens[s] = across(value, 1)
            tables[s] = table_of(chosen)

    riding = aligned and len(groups) > 2
    half = heads // 2
    choices, arrived, finished, back = {}, {}, {}, {}
    sent_out(groups[1], [])
    arrived[0] = dispatched(groups[0], True)
    probs, attended, folded_a = forward((0, half), [])
    brought(groups[1], [])
    if len(groups) > 2:
        sent_out(groups[2], [tokens[s] for s in groups[1]])
    arrived[1] = dispatched(groups[1], True)
    finished[0] = worked(groups[0], arrived[0], True)
    probs, attended, folded_b = forward((half, heads - half), [probs, attended])
    if len(groups) > 2:
        brought(groups[2], [])
        arrived[2] = dispatched(groups[2], True, [folded_a, folded_b] if riding else [])
    for n in range(1, len(groups)):
        finished[n] = worked(groups[n], arrived[n], n == 2)
        rows = finished[n][0]
        if n == 1:
            back[1] = exchanged(rows)
        else:
            back[2] = exchanged(rows)
    held, _ = lax.optimization_barrier((finished[0][0], back[max(back)]))
    back[0] = exchanged(held)

    def sent_home(group, totals, via):
        totals = {s: total.astype(jnp.bfloat16) for s, total in zip(group, totals)}
        return [shift(total, -via.get(s, s)) for s, total in totals.items()]

    totals = combined(groups[1], back[1])
    relayed = grp_count == 4
    if relayed:
        waiting = totals.pop(groups[1].index(1))
    sums = sent_home([s for s in groups[1] if s != 1 or not relayed], totals, {})
    if len(groups) > 2:
        back[0], sums = lax.optimization_barrier((back[0], sums))
        sums += sent_home(groups[2], combined(groups[2], back[2]), {2: 1} if relayed else {})
    own_sum = combined(groups[0], back[0])[0]
    if relayed:
        waiting, _ = lax.optimization_barrier((waiting, last))
        passed = (waiting + sums.pop().astype(jnp.float32)).astype(jnp.bfloat16)
        sums.append(shift(passed, -1))
        last[:] = lax.optimization_barrier((last, passed))[0]
    sums.append(own_sum)
    grad_first, grad_second = adapter_gradients(
        place, [finished[k][1] for k in finished], down_first_factor[0], cells, pairs, last
    )
    last[:] = [grad_first]

    if riding:
        folded = jnp.sum(arrived[2][0][:, cells * len(groups[2]) :].astype(jnp.float32), axis=0)
        folded = folded.reshape(folded.shape[0], 2, -1, tok_rows).transpose(1, 2, 0, 3)
        folded = folded.reshape(2, -1, tok_rows)
        folded = folded[0] + across(folded[1].astype(jnp.bfloat16), 1).astype(jnp.float32)
    else:
        folded = (folded_a + folded_b).astype(jnp.bfloat16)
        folded = lax.all_to_all(folded, "dev", 0, 0, tiled=True)
        folded = jnp.sum(folded.astype(jnp.float32), axis=0)
    folded = folded.astype(jnp.bfloat16)

    residual, near = residual_messages(place, output_gradient, sums, folded, pairs, last)
    near = near[:1] + [across(near[j], 2 * j) for j in range(1, pairs)]
    grads, term, columns = head_gradients(
        place,
        [0],
        near[:1],
        [across(near[0], 1)],
        output_weight,
        output_first_factor,
        output_second_factor,
        attended,
        pairs,
        last,
    )
    last[:] = grads
    held, _ = lax.optimization_barrier((near[1:], last))
    more, row_term, mine = head_gradients(
        place,
        list(range(1, pairs)),
        held,
        [across(part, 1) for part in held],
        output_weight,
        output_first_factor,
        output_second_factor,
        attended,
        pairs,
        last,
    )
    last[:] = more[:1]
    grads += more
    row_term = row_term + term
    mine = (mine + columns).astype(jnp.bfloat16)
    rank, share = mine.shape
    chip = dev_index // 2

    row_term = row_term.astype(jnp.bfloat16)
    if row_term.shape == mine.shape:
        terms = jnp.concatenate([row_term, mine], axis=0)
        terms = planes_sum([terms] + [shift(terms, s) for s in range(1, grp_count)], grp_index)
        output_first_gradient, mine = terms[:rank], terms[rank:]
    else:
        output_first_gradient = planes_sum(
            [row_term] + [shift(row_term, s) for s in range(1, grp_count)], grp_index
        )
        mine = planes_sum([mine] + [shift(mine, s) for s in range(1, grp_count)], grp_index)
    mine = mine.astype(jnp.bfloat16)

    query_gradient, pair_even, pair_odd = attention_backward(
        place,
        rotated_queries,
        rotated_keys,
        stored_values,
        attended,
        probs,
        grads,
        tok_rows,
        last,
    )
    both = (pair_even + across(pair_odd, 1).astype(jnp.float32)).astype(jnp.bfloat16)
    lanes = both.shape[2]
    flat = mine.reshape(rank * share // lanes, lanes)
    ends = [jnp.concatenate([both[j], flat], axis=0) for j in range(pairs)]
    ends = [ends[0]] + [across(ends[j], 2 * j) for j in range(1, pairs)]
    grads = []
    for group in range(KVH):
        grad = jnp.zeros((tok_rows, lanes), jnp.float32)
        for j in range(pairs):
            here = (dev_index ^ (2 * j)) * heads // group_size == group
            grad = grad + jnp.where(here, ends[j][:tok_rows].astype(jnp.float32), 0.0)
        grads.append(grad)
    key_gradient = jnp.concatenate([grad[:, :HEAD_SIZE] for grad in grads], axis=1)
    value_gradient = jnp.concatenate([grad[:, HEAD_SIZE:] for grad in grads], axis=1)
    second_columns = []
    for number in range(pairs):
        part = jnp.zeros((rank, share), jnp.float32)
        for j in range(pairs):
            value = ends[j][tok_rows:].astype(jnp.float32).reshape(rank, share)
            part = part + jnp.where(chip ^ j == number, value, 0.0)
        second_columns.append(part)
    output_second_gradient = jnp.concatenate(second_columns, axis=1)
    return (
        grad_first[None],
        grad_second[None],
        residual,
        output_first_gradient,
        output_second_gradient,
        query_gradient,
        key_gradient,
        value_gradient,
    )


def solution(mesh):
    in_specs = (
        P(("grp", "dev"), None),
        P(("grp", "dev"), None),
        P(("grp", "dev"), None),
        P(("grp", "dev"), None, None),
        P(("grp", "dev"), None, None),
        P(("grp", "dev"), None, None),
        P(("grp", "dev"), None, None),
        P(("grp", "dev"), None, None),
        P("grp", "dev"),
        P("grp", None),
        P("grp", None),
        P("dev", None),
        P(None, "dev"),
        P(),
    )
    out_specs = (
        P(("grp", "dev"), None, None),
        P(("grp", "dev"), None, None),
        P(("grp", "dev"), None),
        P(None, "dev"),
        P(),
        P("grp", "dev"),
        P(("grp", "dev"), None),
        P(("grp", "dev"), None),
    )
    return jax.shard_map(
        on_device, mesh=mesh, in_specs=in_specs, out_specs=out_specs, check_vma=False
    )
```
